256 devices in a mesh: lat: 32 (over x_hi, z, core), chan: 8 (over y, x_lo).
Axes of the slice: x: 4 (x_hi: 2, x_lo: 2; x = x_hi * 2 + x_lo), y: 4, z: 8, core: 2. Of those that a mesh axis runs over, the one named last changes fastest.
Arguments:
- fields: bfloat16 [6, 96, 192, 768], P(None, 'lat', None, 'chan'), may hold values from -60 to 60, as said below
- kept_lat: int32 [4], replicated, may hold values from 0 to 5, as said below
- kept_lon: int32 [4], replicated, may hold values from 0 to 5, as said below
- spec_w1: bfloat16 [2, 8, 96, 96], P(None, 'chan'), may hold values from -0.4375 to 0.4375
- spec_w2: bfloat16 [2, 8, 96, 96], P(None, 'chan'), may hold values from -0.4375 to 0.4375
- mlp_w1: bfloat16 [768, 3072], replicated, may hold values from -0.21875 to 0.21875
- mlp_w2: bfloat16 [3072, 768], replicated, may hold values from -0.109375 to 0.109375
Outputs:
- block_out: bfloat16 [6, 96, 192, 768], P(None, 'lat', None, 'chan')
The draws below stay inside these ranges and needn't reach their ends.
Inputs may be any that keep to these rules, and one draw needn't show every extreme that they name: `fields`: finite values. `kept_lat`: 4 distinct block numbers in rising order, always holding 0 and 5. `kept_lon`: 4 distinct block numbers in rising order, always holding 0 and 5.
All inputs are finite; a program needn't handle non-finite values.
Results may differ from the reference program's by a relative error of at most 0.0065.
Values may be sent and summed in bfloat16 or wider, within the bound.
A program may use at most 128 MiB of HBM per device.

```python
import math
import jax
import jax.numpy as jnp
from jax import lax

S = 6
H = 96
W = 192
C = 768
NB = 8
HID = 3072
MB = 16
KBL = 4
KBW = 4
BS = 96
NBL = 6
NBW = 6
KL = 64
KW = 64


def draw_fields(key, part):
    key_base, key_chan, key_token = jax.random.split(key, 3)
    channel_ids = jnp.arange(C, dtype=jnp.float32)
    chan_scale = 10.0 ** (channel_ids / C - 0.5) * jax.random.uniform(key_chan, (C,), jnp.float32, 0.7, 1.4)
    token_scale = 10.0 ** jax.random.uniform(key_token, (S, H, W, 1), jnp.float32, -0.5, 0.5)
    base_draw = jnp.clip(jax.random.normal(key_base, (S, H, W, C), jnp.float32), -4.0, 4.0)
    values = base_draw * token_scale * chan_scale
    return values.astype(jnp.bfloat16)


def pick_blocks(key, block_total, block_count):
    middle_part = jax.random.permutation(key, block_total - 2).astype(jnp.int32) + 1
    chosen = jnp.concatenate([jnp.zeros((1,), jnp.int32), middle_part[:block_count - 2], jnp.full((1,), block_total - 1, jnp.int32)])
    return jnp.sort(chosen)


def draw_kept_lat(key, part):
    return pick_blocks(jax.random.fold_in(key, 11), NBL, KBL)


def draw_kept_lon(key, part):
    return pick_blocks(jax.random.fold_in(key, 23), NBW, KBW)


def level_of(own_key, shape, cuts, smallest, largest):
    gain = 1.0
    for axis_at, blocks in cuts:
        steps = jax.random.uniform(jax.random.fold_in(jax.random.fold_in(own_key, 6), axis_at), (blocks,), jnp.float32, smallest / len(cuts), largest / len(cuts))
        gain = gain * jnp.repeat(jnp.exp(steps), shape[axis_at] // blocks).reshape((-1,) + (1,) * (len(shape) - 1 - axis_at))
    return gain


def noise(rng, shape, deviation, reach, cuts=(), held_as=jnp.bfloat16):
    loudness = level_of(rng, shape, cuts, -0.22, 0.18) if cuts else 1.0
    drawn = jax.random.normal(rng, shape, jnp.float32) * deviation * loudness
    return jnp.minimum(jnp.maximum(drawn, -reach), reach).astype(held_as)


def setup_inputs(seed: int = 0) -> dict:
    arg_keys = jax.random.split(jax.random.key(seed), 8)
    return {
        "fields": draw_fields(jax.random.fold_in(arg_keys[7], 71), 0),
        "kept_lat": draw_kept_lat(jax.random.fold_in(arg_keys[7], 71), 0),
        "kept_lon": draw_kept_lon(jax.random.fold_in(arg_keys[7], 71), 0),
        "spec_w1": noise(arg_keys[3], (2, NB, BS, BS), (2 * BS) ** -0.5, 0.4375, ((1, 8),)),
        "spec_w2": noise(arg_keys[4], (2, NB, BS, BS), (2 * BS) ** -0.5, 0.4375, ((1, 8),)),
        "mlp_w1": noise(arg_keys[5], (C, HID), C ** -0.5, 0.21875),
        "mlp_w2": noise(arg_keys[6], (HID, C), HID ** -0.5, 0.109375),
    }


norm_eps = 1e-05

def mode_list(kept_blocks, block_width):
    offsets = jnp.arange(block_width, dtype=jnp.int32)
    return (kept_blocks.astype(jnp.int32)[:, None] * block_width + offsets[None, :]).reshape(-1)

def lon_forward_table(lon_waves, span_size):
    positions = jnp.arange(span_size, dtype=jnp.int32)
    angle = 2.0 * math.pi / span_size * jnp.mod(positions[:, None] * lon_waves[None, :], span_size).astype(jnp.float32)
    factor = 1.0 / math.sqrt(span_size)
    return jnp.stack([jnp.cos(angle) * factor, -jnp.sin(angle) * factor], axis=1).astype(jnp.bfloat16)

def lon_inverse_table(lon_waves, span_size):
    positions = jnp.arange(span_size, dtype=jnp.int32)
    angle = 2.0 * math.pi / span_size * jnp.mod(lon_waves[:, None] * positions[None, :], span_size).astype(jnp.float32)
    factor = jnp.where(lon_waves > 0, 2.0, 1.0).astype(jnp.float32)[:, None] / math.sqrt(span_size)
    return jnp.stack([jnp.cos(angle) * factor, -jnp.sin(angle) * factor], axis=1).astype(jnp.bfloat16)

def lat_forward_table(lat_waves, row_ids, height):
    angle = 2.0 * math.pi / height * jnp.mod(lat_waves[:, None] * row_ids[None, :], height).astype(jnp.float32)
    cosine = jnp.cos(angle) / math.sqrt(height)
    sine = jnp.sin(angle) / math.sqrt(height)
    upper = jnp.stack([cosine, sine], axis=-1)
    lower = jnp.stack([-sine, cosine], axis=-1)
    return jnp.stack([upper, lower], axis=1).astype(jnp.bfloat16)

def lat_inverse_table(row_ids, lat_waves, height):
    angle = 2.0 * math.pi / height * jnp.mod(row_ids[:, None] * lat_waves[None, :], height).astype(jnp.float32)
    cosine = jnp.cos(angle) / math.sqrt(height)
    sine = jnp.sin(angle) / math.sqrt(height)
    upper = jnp.stack([cosine, -sine], axis=-1)
    lower = jnp.stack([sine, cosine], axis=-1)
    return jnp.stack([upper, lower], axis=1).astype(jnp.bfloat16)

def complex_weight(weights):
    real_part = weights[0]
    imag_part = weights[1]
    return jnp.stack([jnp.stack([real_part, imag_part], axis=2), jnp.stack([-imag_part, real_part], axis=2)], axis=0)

def spectral_filter(modes, weight_one, weight_two):
    layer_one = jnp.einsum('kmsni,snioj->kmonj', modes.astype(jnp.float32), complex_weight(weight_one).astype(jnp.float32))
    layer_one = jnp.maximum(layer_one, 0.0).astype(jnp.bfloat16)
    layer_two = jnp.einsum('kmsni,snioj->kmonj', layer_one.astype(jnp.float32), complex_weight(weight_two).astype(jnp.float32))
    return layer_two.astype(jnp.bfloat16)

def layer_norm(values):
    average = lax.optimization_barrier(jnp.mean(values, axis=-1, keepdims=True))
    spread = lax.optimization_barrier(jnp.mean(values * values, axis=-1, keepdims=True)) - average * average
    return (values - average) * lax.rsqrt(spread + norm_eps)

def reference(fields, kept_lat, kept_lon, spec_w1, spec_w2, mlp_w1, mlp_w2):
    lat_waves = mode_list(kept_lat, MB)
    lon_waves = mode_list(kept_lon, MB)
    row_ids = jnp.arange(H, dtype=jnp.int32)
    forward_lon = lon_forward_table(lon_waves, W).astype(jnp.float32)
    inverse_lon = lon_inverse_table(lon_waves, W).astype(jnp.float32)
    forward_lat = lat_forward_table(lat_waves, row_ids, H).astype(jnp.float32)
    inverse_lat = lat_inverse_table(row_ids, lat_waves, H).astype(jnp.float32)

    def section_one(block_rows):
        normed = layer_norm(block_rows.astype(jnp.float32)).astype(jnp.bfloat16)
        return jnp.einsum('hwc,wsm->hmsc', normed.astype(jnp.float32), forward_lon).astype(jnp.bfloat16)

    def section_two(inputs_pair):
        block_rows, wave_rows = inputs_pair
        field_values = block_rows.astype(jnp.float32)
        normed = layer_norm(field_values).astype(jnp.bfloat16)
        spectral = jnp.einsum('hmsc,msw->hwc', wave_rows.astype(jnp.float32), inverse_lon)
        mixed = (field_values + normed.astype(jnp.float32) + spectral).astype(jnp.bfloat16)
        normed_two = layer_norm(mixed.astype(jnp.float32)).astype(jnp.bfloat16)
        hidden = jax.nn.gelu(jnp.dot(normed_two.reshape(-1, C), mlp_w1, preferred_element_type=jnp.float32), approximate=False).astype(jnp.bfloat16)
        result = mixed.astype(jnp.float32).reshape(-1, C) + jnp.dot(hidden, mlp_w2, preferred_element_type=jnp.float32)
        return result.astype(jnp.bfloat16).reshape(8, W, C)

    def one_sample(sample_fields):
        row_blocks = sample_fields.reshape(H // 8, 8, W, C)
        along = lax.map(section_one, row_blocks).reshape(H, KW, 2, C)
        spectrum = jnp.einsum('kohs,hmsc->kmoc', forward_lat, along.astype(jnp.float32)).astype(jnp.bfloat16)
        filtered = spectral_filter(spectrum.reshape(KL, KW, 2, NB, BS), spec_w1, spec_w2).reshape(KL, KW, 2, C)
        wave = jnp.einsum('hoks,kmsc->hmoc', inverse_lat, filtered.astype(jnp.float32)).astype(jnp.bfloat16)
        block_out = lax.map(section_two, (row_blocks, wave.reshape(H // 8, 8, KW, 2, C)))
        return block_out.reshape(H, W, C)
    return lax.map(one_sample, fields)
```

```python
import math

import jax
import jax.numpy as jnp
import numpy as np
from jax import lax
from jax.experimental import pallas as pl
from jax.experimental.pallas import tpu as pltpu
from jax.sharding import PartitionSpec as P

S, H, W, C, HID, BS = 6, 96, 192, 768, 3072, 96
L, NC = 32, 8
RH = H // L
NCH = 2
SC = S // NCH
NR = SC * RH
WS = W // NC
CELLS = 224
GRP = CELLS // 4
PACKED = 176
EPS = 1e-5
F32, BF16 = jnp.float32, jnp.bfloat16
MESH = pl.DeviceIdType.MESH


def tables():
    k = np.arange(96)
    w = np.arange(W)
    angle = 2.0 * np.pi / W * ((k[:, None] * w[None, :]) % W)
    fwd = np.stack([np.cos(angle), -np.sin(angle)]) / math.sqrt(W)
    gain = np.where(k > 0, 2.0, 1.0)[:, None] / math.sqrt(W)
    inv = np.zeros((2, 96, 256))
    inv[:, :, :W] = np.stack([np.cos(angle) * gain, -np.sin(angle) * gain])
    h = (np.arange(L)[None, :] * RH + np.arange(RH)[:, None]).reshape(-1)
    angle = 2.0 * np.pi / H * ((k[:, None] * h[None, :]) % H)
    lat = np.zeros((2, 96, 128))
    lat[:, :, :H] = np.stack([np.cos(angle), np.sin(angle)]) / math.sqrt(H)
    cast = lambda t: jnp.asarray(t.reshape(2, 6, 16, -1).astype(np.float32), dtype=BF16)
    return cast(fwd), cast(inv), cast(lat)


def lanes(rows):
    return lax.broadcasted_iota(jnp.int32, (rows, 128), 1)


def fold(a0, a1, a2, a3):
    low = lanes(a0.shape[0]) < BS
    return (
        jnp.where(low, a0, pltpu.roll(a3, 96, 1)),
        jnp.where(low, a1, pltpu.roll(a3, 64, 1)),
        jnp.where(low, a2, pltpu.roll(a3, 32, 1)),
    )


def fourth(t0, t1, t2):
    lane = lanes(t0.shape[0])
    return jnp.where(
        lane < 32,
        pltpu.roll(t0, 32, 1),
        jnp.where(lane < 64, pltpu.roll(t1, 64, 1), pltpu.roll(t2, 96, 1)),
    )


def dot(a, b):
    return jnp.dot(a, b, preferred_element_type=F32)


def fold_cells(m):
    parts = fold(*(m[g * GRP : (g + 1) * GRP] for g in range(4)))
    pad = jnp.zeros((PACKED - 3 * GRP, 128), F32)
    return jnp.concatenate(list(parts) + [pad], axis=0).astype(BF16)


def unfold_cells(t):
    t = t.astype(F32)
    parts = [t[g * GRP : (g + 1) * GRP] for g in range(3)]
    y = jnp.concatenate(parts + [fourth(*parts)], axis=0)
    return jnp.where(lanes(CELLS) < BS, y, 0.0)


def gelu(u):
    return 0.5 * u * (1.0 + lax.erf(u * (1.0 / math.sqrt(2.0))))


def kernel(
    kept_lat,
    kept_lon,
    x_ref,
    sw1,
    sw2,
    ftab,
    gtab,
    ltab,
    w1_hbm,
    w2_hbm,
    out_ref,
    fmat,
    gmat,
    cs,
    ct,
    sf1,
    sf2,
    w1v,
    w2v,
    stat_send,
    stat_recv,
    stat_scr,
    nrm,
    a_scr,
    f_send,
    f_recv,
    r_scr,
    b_scr,
    sp,
    fi,
    b_send,
    b_recv,
    m_scr,
    c_send,
    c_recv,
    y_scr,
    n2,
    hid,
    d_send,
    d_recv,
    o_scr,
    wsem,
    ssem,
    rsem,
):
    lat = lax.axis_index("lat")
    chan = lax.axis_index("chan")

    loads = []
    for s in range(NC):
        loads.append(
            pltpu.make_async_copy(
                w1_hbm.at[pl.ds(s * BS, BS)], w1v.at[pl.ds(s * 128, BS)], wsem.at[s]
            )
        )
    loads.append(pltpu.make_async_copy(w2_hbm, w2v, wsem.at[NC]))
    for c in loads:
        c.start()

    barrier = pltpu.get_barrier_semaphore()

    def greet_lat(i, carry):
        pl.semaphore_signal(
            barrier, inc=1, device_id=(lax.rem(lat + i, L), chan), device_id_type=MESH
        )
        return carry

    def greet_chan(i, carry):
        pl.semaphore_signal(
            barrier, inc=1, device_id=(lat, lax.rem(chan + i, NC)), device_id_type=MESH
        )
        return carry

    lax.fori_loop(1, L, greet_lat, 0)
    lax.fori_loop(1, NC, greet_chan, 0)

    def spread_lat(src, dst, phase, k):
        pltpu.make_async_copy(src.at[k, lat], dst.at[k, lat], rsem.at[phase, k]).start()

        def go(i, carry):
            to = lax.rem(lat + i, L)
            pltpu.make_async_remote_copy(
                src_ref=src.at[k, to],
                dst_ref=dst.at[k, lat],
                send_sem=ssem.at[phase, k],
                recv_sem=rsem.at[phase, k],
                device_id=(to, chan),
                device_id_type=MESH,
            ).start()
            return carry

        lax.fori_loop(1, L, go, 0)

    def spread_chan(src, dst, phase, k, same):
        own = src.at[k, 0] if same else src.at[k, chan]
        pltpu.make_async_copy(own, dst.at[k, chan], rsem.at[phase, k]).start()

        def go(i, carry):
            to = lax.rem(chan + i, NC)
            pltpu.make_async_remote_copy(
                src_ref=src.at[k, 0] if same else src.at[k, to],
                dst_ref=dst.at[k, chan],
                send_sem=ssem.at[phase, k],
                recv_sem=rsem.at[phase, k],
                device_id=(lat, to),
                device_id_type=MESH,
            ).start()
            return carry

        lax.fori_loop(1, NC, go, 0)

    def arrived(dst, phase, k):
        pltpu.make_async_copy(dst.at[k], dst.at[k], rsem.at[phase, k]).wait()

    def sent(dst, phase, k, count):
        part = dst.at[k, pl.ds(0, count)]
        pltpu.make_async_copy(part, part, ssem.at[phase, k]).wait()

    ones = jnp.ones((8, BS), BF16)
    rows_dot = lambda b: lax.dot_general(
        ones, b, (((1,), (1,)), ((), ())), preferred_element_type=F32
    )
    stat_send[...] = jnp.zeros_like(stat_send)
    for k in range(NCH):
        for r in range(NR):
            xr = x_ref[pl.ds((k * NR + r) * W, W), :]
            xf = xr.astype(F32)
            sq = xf * xf
            hi = sq.astype(BF16)
            lo = (sq - hi.astype(F32)).astype(BF16)
            stat_send[k, 0, pl.ds(r, 1), pl.ds(0, W)] = rows_dot(xr)[0:1]
            stat_send[k, 0, pl.ds(NR + r, 1), pl.ds(0, W)] = (rows_dot(hi) + rows_dot(lo))[0:1]
        if k == 0:
            pl.semaphore_wait(barrier, L - 1 + NC - 1)
        spread_chan(stat_send, stat_recv, 0, k, True)

    for q in range(4):
        for b in range(2):
            blk = kept_lon[(q // 2) * 2 + b]
            fmat[pl.ds(q * 32 + b * 16, 16), :] = ftab[q % 2, blk]
    g = jnp.concatenate(
        [gtab[q % 2, kept_lon[(q // 2) * 2 + b]].astype(F32) for q in range(4) for b in range(2)],
        axis=0,
    )
    gmat[...] = g.T[0:W].astype(BF16)
    t = jnp.concatenate([ltab[q, kept_lat[b]].astype(F32) for q in range(2) for b in range(4)], axis=0)
    cs[...] = t.astype(BF16)
    ct[...] = t.T[0:H].astype(BF16)
    for src, dst in ((sw1, sf1), (sw2, sf2)):
        dst[...] = jnp.zeros_like(dst)
        real, imag = src[0], src[1]
        dst[pl.ds(0, BS), pl.ds(0, BS)] = real
        dst[pl.ds(0, BS), pl.ds(128, BS)] = imag
        dst[pl.ds(128, BS), pl.ds(0, BS)] = -imag
        dst[pl.ds(128, BS), pl.ds(128, BS)] = real
    nrm[...] = jnp.zeros_like(nrm)
    a_scr[...] = jnp.zeros_like(a_scr)
    m_scr[...] = jnp.zeros_like(m_scr)
    stat_scr[...] = jnp.zeros_like(stat_scr)
    for s in range(NC):
        w1v[pl.ds(s * 128 + BS, 32), :] = jnp.zeros((32, HID), BF16)

    def regroup(k, dst):
        for d in range(L):
            dst[k, d] = a_scr[pl.ds(d, 32, stride=32), :].astype(BF16)

    for k in range(NCH):
        arrived(stat_recv, 0, k)
        tot = stat_recv[k, 0]
        for s in range(1, NC):
            tot = tot + stat_recv[k, s]
        tot = tot * (1.0 / C)
        mean = tot[0:NR]
        var = tot[NR : 2 * NR] - mean * mean
        stat_scr[pl.ds(0, NR), :] = mean
        stat_scr[pl.ds(16, NR), :] = lax.rsqrt(var + EPS)
        stat = stat_scr[...].T
        for r in range(NR):
            at = pl.ds((k * NR + r) * W, W)
            xf = x_ref[at, :].astype(F32)
            normed = ((xf - stat[0:W, r : r + 1]) * stat[0:W, 16 + r : 17 + r]).astype(BF16)
            nrm[at, pl.ds(0, BS)] = normed
            al = dot(fmat[...], nrm[at, :])
            parts = fold(*(al[q * 32 : (q + 1) * 32] for q in range(4)))
            for p in range(3):
                a_scr[pl.ds((r * 3 + p) * 32, 32), :] = parts[p]
        regroup(k, f_send)
        spread_lat(f_send, f_recv, 1, k)

    for k in range(NCH):
        arrived(f_recv, 1, k)
        for s in range(L):
            r_scr[pl.ds(s * 32, 32), :] = f_recv[k, s].astype(F32)
        for n in range(SC):
            for hh in range(RH):
                for p in range(3):
                    row = (n * RH + hh) * 3 + p
                    b_scr[pl.ds(hh * 32, 32), pl.ds(p * 128, 128)] = r_scr[
                        pl.ds(row, 32, stride=32), :
                    ].astype(BF16)
            both = dot(cs[:, 0:H], b_scr[...])
            co = [both[0:64, p * 128 : (p + 1) * 128] for p in range(3)]
            si = [both[64:128, p * 128 : (p + 1) * 128] for p in range(3)]
            co.append(fourth(*co))
            si.append(fourth(*si))
            for m in range(2):
                rows = pl.ds((n * 2 + m) * 64, 64)
                sp[rows, pl.ds(0, 128)] = (co[2 * m] + si[2 * m + 1]).astype(BF16)
                sp[rows, pl.ds(128, 128)] = (co[2 * m + 1] - si[2 * m]).astype(BF16)
        one = jnp.maximum(dot(sp[...], sf1[...]), 0.0).astype(BF16)
        fi[...] = dot(one, sf2[...]).astype(BF16)
        for n in range(SC):
            wave = []
            for m in range(2):
                f = fi[pl.ds((n * 2 + m) * 64, 64), :]
                turned = jnp.concatenate([-f[:, 128:256], f[:, 0:128]], axis=1)
                wv = dot(ct[...], jnp.concatenate([f, turned], axis=0))
                wave += [wv[:, 0:128], wv[:, 128:256]]
            parts = fold(*wave)
            for hh in range(RH):
                for p in range(3):
                    a_scr[pl.ds(((n * RH + hh) * 3 + p) * 32, 32), :] = parts[p][
                        hh * 32 : (hh + 1) * 32
                    ]
        regroup(k, b_send)
        spread_lat(b_send, b_recv, 2, k)

    for k in range(NCH):
        arrived(b_recv, 2, k)
        for s in range(L):
            r_scr[pl.ds(s * 32, 32), :] = b_recv[k, s].astype(F32)
        for r in range(NR):
            parts = [r_scr[pl.ds(r * 3 + p, 32, stride=32), :] for p in range(3)]
            wave = jnp.concatenate(parts + [fourth(*parts)], axis=0).astype(BF16)
            spectral = dot(gmat[...], wave)
            at = pl.ds((k * NR + r) * W, W)
            mixed = x_ref[at, :].astype(F32) + nrm[at, pl.ds(0, BS)].astype(F32) + spectral[:, 0:BS]
            for d in range(NC):
                m_scr[d, pl.ds(r * WS, WS), pl.ds(0, BS)] = mixed[d * WS : (d + 1) * WS]
        for d in range(NC):
            c_send[k, d] = fold_cells(m_scr[d])
        spread_chan(c_send, c_recv, 3, k, False)

    for c in loads:
        c.wait()
    for k in range(NCH):
        arrived(c_recv, 3, k)
        acc = jnp.zeros((CELLS, 128), F32)
        acc2 = jnp.zeros((CELLS, 128), F32)
        for s in range(NC):
            y = unfold_cells(c_recv[k, s])
            y_scr[s] = y
            acc = acc + y
            acc2 = acc2 + y * y
        mean = jnp.sum(acc, axis=1, keepdims=True) * (1.0 / C)
        var = jnp.sum(acc2, axis=1, keepdims=True) * (1.0 / C) - mean * mean
        scale = lax.rsqrt(var + EPS)
        for s in range(NC):
            n2[:, pl.ds(s * 128, 128)] = ((y_scr[s] - mean) * scale).astype(BF16)

        def first(i, carry):
            cols = pl.ds(pl.multiple_of(i * 512, 512), 512)
            hid[:, cols] = gelu(dot(n2[...], w1v[:, cols])).astype(BF16)
            return carry

        lax.fori_loop(0, HID // 512, first, 0)
        o = dot(hid[...], w2v[...])
        tiles = [o[:, i * 128 : (i + 1) * 128] for i in range(6)]
        for s in range(NC):
            i, off = divmod(s * BS, 128)
            piece = tiles[i]
            if off:
                piece = pltpu.roll(piece, 128 - off, 1)
                if off > 32:
                    after = pltpu.roll(tiles[i + 1], 128 - off, 1)
                    piece = jnp.where(lanes(CELLS) < 128 - off, piece, after)
            d_send[k, s] = fold_cells(y_scr[s] + piece)
        spread_chan(d_send, d_recv, 4, k, False)

    for k in range(NCH):
        arrived(d_recv, 4, k)
        for s in range(NC):
            y = unfold_cells(d_recv[k, s])
            for r in range(NR):
                o_scr[pl.ds(r * W + s * WS, WS), :] = y[r * WS : (r + 1) * WS]
        out_ref[pl.ds(k * NR * W, NR * W), :] = o_scr[:, 0:BS].astype(BF16)

    for k in range(NCH):
        sent(stat_recv, 0, k, NC - 1)
        sent(f_send, 1, k, L - 1)
        sent(b_send, 2, k, L - 1)
        sent(c_send, 3, k, NC - 1)
        sent(d_send, 4, k, NC - 1)


def on_device(fields, kept_lat, kept_lon, spec_w1, spec_w2, mlp_w1, mlp_w2):
    fwd, inv, lat = tables()
    vmem = pl.BlockSpec(memory_space=pltpu.VMEM)
    smem = pl.BlockSpec(memory_space=pltpu.SMEM)
    hbm = pl.BlockSpec(memory_space=pl.ANY)
    cells = S * RH * W
    out = pl.pallas_call(
        kernel,
        out_shape=jax.ShapeDtypeStruct((cells, BS), BF16),
        in_specs=[smem, smem, vmem, vmem, vmem, vmem, vmem, vmem, hbm, hbm],
        out_specs=vmem,
        scratch_shapes=[
            pltpu.VMEM((128, W), BF16),
            pltpu.VMEM((W, 128), BF16),
            pltpu.VMEM((128, 128), BF16),
            pltpu.VMEM((H, 128), BF16),
            pltpu.VMEM((256, 256), BF16),
            pltpu.VMEM((256, 256), BF16),
            pltpu.VMEM((NC * 128, HID), BF16),
            pltpu.VMEM((HID, C), BF16),
            pltpu.VMEM((NCH, 1, 24, 256), F32),
            pltpu.VMEM((NCH, NC, 24, 256), F32),
            pltpu.VMEM((128, 256), F32),
            pltpu.VMEM((cells, 128), BF16),
            pltpu.VMEM((1024, 128), F32),
            pltpu.VMEM((NCH, L, 32, 128), BF16),
            pltpu.VMEM((NCH, L, 32, 128), BF16),
            pltpu.VMEM((1024, 128), F32),
            pltpu.VMEM((H, 384), BF16),
            pltpu.VMEM((SC * 128, 256), BF16),
            pltpu.VMEM((SC * 128, 256), BF16),
            pltpu.VMEM((NCH, L, 32, 128), BF16),
            pltpu.VMEM((NCH, L, 32, 128), BF16),
            pltpu.VMEM((NC, CELLS, 128), F32),
            pltpu.VMEM((NCH, NC, PACKED, 128), BF16),
            pltpu.VMEM((NCH, NC, PACKED, 128), BF16),
            pltpu.VMEM((NC, CELLS, 128), F32),
            pltpu.VMEM((CELLS, NC * 128), BF16),
            pltpu.VMEM((CELLS, HID), BF16),
            pltpu.VMEM((NCH, NC, PACKED, 128), BF16),
            pltpu.VMEM((NCH, NC, PACKED, 128), BF16),
            pltpu.VMEM((NR * W, 128), F32),
            pltpu.SemaphoreType.DMA((NC + 1,)),
            pltpu.SemaphoreType.DMA((5, NCH)),
            pltpu.SemaphoreType.DMA((5, NCH)),
        ],
        compiler_params=pltpu.CompilerParams(
            collective_id=0, has_side_effects=True, vmem_limit_bytes=56 * 1024 * 1024
        ),
        cost_estimate=pl.CostEstimate(
            flops=5_000_000_000, bytes_accessed=12_000_000, transcendentals=1_400_000
        ),
    )(
        kept_lat,
        kept_lon,
        fields.reshape(cells, BS),
        spec_w1.reshape(2, BS, BS),
        spec_w2.reshape(2, BS, BS),
        fwd,
        inv,
        lat,
        mlp_w1,
        mlp_w2,
    )
    return out.reshape(S, RH, W, BS)


def solution(mesh):
    placed = (
        P(None, "lat", None, "chan"),
        P(),
        P(),
        P(None, "chan", None, None),
        P(None, "chan", None, None),
        P(),
        P(),
    )
    return jax.shard_map(
        on_device,
        mesh=mesh,
        in_specs=placed,
        out_specs=P(None, "lat", None, "chan"),
        check_vma=False,
    )
```

```python
import math

import jax
import jax.numpy as jnp
import numpy as np
from jax import lax
from jax.experimental import pallas as pl
from jax.experimental.pallas import tpu as pltpu
from jax.sharding import PartitionSpec as P

S, H, W, C, HID, BS = 6, 96, 192, 768, 3072, 96
L, NC = 32, 8
RH = H // L
NCH = 2
SC = S // NCH
NR = SC * RH
WS = W // NC
BOUNDS = (0, 8, 14, 18)
NT = len(BOUNDS) - 1
CUTS = {
    8: (0, 48, 96, 144, 192),
    6: (0, 40, 80, 112, 144),
    4: (0, 32, 56, 80, 96),
}
ROWS = [BOUNDS[j + 1] - BOUNDS[j] for j in range(NT)]
PACKED = [CUTS[n][3] for n in ROWS]
MAXC, MAXP = max(ROWS) * WS, max(PACKED)
TH = 64
TR = W // TH
EPS = 1e-5
F32, BF16 = jnp.float32, jnp.bfloat16
MESH = pl.DeviceIdType.MESH


def tables():
    k = np.arange(96)
    w = np.arange(W)
    angle = 2.0 * np.pi / W * ((k[:, None] * w[None, :]) % W)
    fwd = np.stack([np.cos(angle), -np.sin(angle)]) / math.sqrt(W)
    gain = np.where(k > 0, 2.0, 1.0)[:, None] / math.sqrt(W)
    inv = np.zeros((2, 96, 256))
    inv[:, :, :W] = np.stack([np.cos(angle) * gain, -np.sin(angle) * gain])
    h = (np.arange(L)[None, :] * RH + np.arange(RH)[:, None]).reshape(-1)
    angle = 2.0 * np.pi / H * ((k[:, None] * h[None, :]) % H)
    lat = np.zeros((2, 96, 128))
    lat[:, :, :H] = np.stack([np.cos(angle), np.sin(angle)]) / math.sqrt(H)
    cast = lambda t: jnp.asarray(t.reshape(2, 6, 16, -1).astype(np.float32), dtype=BF16)
    return cast(fwd), cast(inv), cast(lat)


def lanes(rows):
    return lax.broadcasted_iota(jnp.int32, (rows, 128), 1)


def fold(a0, a1, a2, a3):
    low = lanes(a0.shape[0]) < BS
    return (
        jnp.where(low, a0, pltpu.roll(a3, 96, 1)),
        jnp.where(low, a1, pltpu.roll(a3, 64, 1)),
        jnp.where(low, a2, pltpu.roll(a3, 32, 1)),
    )


def fourth(t0, t1, t2):
    lane = lanes(t0.shape[0])
    return jnp.where(
        lane < 32,
        pltpu.roll(t0, 32, 1),
        jnp.where(lane < 64, pltpu.roll(t1, 64, 1), pltpu.roll(t2, 96, 1)),
    )


def dot(a, b):
    return jnp.dot(a, b, preferred_element_type=F32)


def fold_cells(m, cuts):
    last = m[cuts[3] : cuts[4]]
    out = []
    for g in range(3):
        here = m[cuts[g] : cuts[g + 1]]
        extra = here.shape[0] - last.shape[0]
        add = jnp.concatenate([last, jnp.zeros((extra, 128), F32)], axis=0) if extra else last
        out.append(jnp.where(lanes(here.shape[0]) < BS, here, pltpu.roll(add, 96 - 32 * g, 1)))
    return jnp.concatenate(out, axis=0).astype(BF16)


def unfold_cells(t, cuts):
    t = t.astype(F32)
    parts = [t[cuts[g] : cuts[g + 1]] for g in range(3)]
    n = cuts[4] - cuts[3]
    return jnp.concatenate(parts + [fourth(*(p[0:n] for p in parts))], axis=0)


def gelu(u):
    return 0.5 * u * (1.0 + lax.erf(u * (1.0 / math.sqrt(2.0))))


def kernel(
    lat_hbm,
    lon_hbm,
    x_hbm,
    sw1_hbm,
    sw2_hbm,
    ftab_hbm,
    gtab_hbm,
    ltab_hbm,
    w1_hbm,
    w2_hbm,
    out_hbm,
    kept_lat,
    kept_lon,
    x_ref,
    sw1,
    sw2,
    ftab,
    gtab,
    ltab,
    fmat,
    gmat,
    cs,
    ct,
    sf1,
    sf2,
    w1v,
    w2v,
    st_part,
    st_in,
    nrm,
    a_scr,
    f_send,
    f_recv,
    r_scr,
    b_scr,
    sp,
    b_send,
    b_recv,
    m_scr,
    c_send,
    c_recv,
    y_scr,
    n2,
    hid,
    d_send,
    d_recv,
    o_scr,
    o_buf,
    wsem,
    isem,
    osem,
    ssem,
    rsem,
):
    lat = lax.axis_index("lat")
    chan = lax.axis_index("chan")

    half = S * RH * W // NCH
    x_loads = [
        pltpu.make_async_copy(
            x_hbm.at[pl.ds(k * half, half)], x_ref.at[pl.ds(k * half, half)], isem.at[k]
        )
        for k in range(NCH)
    ]
    small = (
        (lat_hbm, kept_lat),
        (lon_hbm, kept_lon),
        (ftab_hbm, ftab),
        (gtab_hbm, gtab),
        (ltab_hbm, ltab),
        (sw1_hbm, sw1),
        (sw2_hbm, sw2),
    )
    s_loads = [
        pltpu.make_async_copy(src, dst, isem.at[NCH + i]) for i, (src, dst) in enumerate(small)
    ]
    loads = [
        pltpu.make_async_copy(w1_hbm, w1v, wsem.at[0]),
        pltpu.make_async_copy(w2_hbm, w2v, wsem.at[1]),
    ]
    for c in x_loads:
        c.start()

    barrier = pltpu.get_barrier_semaphore()

    def greet_lat(i, carry):
        pl.semaphore_signal(
            barrier, inc=1, device_id=(lax.rem(lat + i, L), chan), device_id_type=MESH
        )
        return carry

    def greet_chan(i, carry):
        pl.semaphore_signal(
            barrier, inc=1, device_id=(lat, lax.rem(chan + i, NC)), device_id_type=MESH
        )
        return carry

    lax.fori_loop(1, L, greet_lat, 0)
    lax.fori_loop(1, NC, greet_chan, 0)
    for c in s_loads + loads:
        c.start()

    def spread_lat(src, dst, phase, k):
        pltpu.make_async_copy(src.at[k, lat], dst.at[k, lat], rsem.at[phase, k]).start()

        def go(i, carry):
            to = lax.rem(lat + i, L)
            pltpu.make_async_remote_copy(
                src_ref=src.at[k, to],
                dst_ref=dst.at[k, lat],
                send_sem=ssem.at[phase, k],
                recv_sem=rsem.at[phase, k],
                device_id=(to, chan),
                device_id_type=MESH,
            ).start()
            return carry

        lax.fori_loop(1, L, go, 0)

    def spread_chan(src, dst, phase, k, rows, same):
        part = pl.ds(0, rows)
        own = src.at[k, 0 if same else chan, part]
        pltpu.make_async_copy(own, dst.at[k, chan, part], rsem.at[phase, k]).start()

        def go(i, carry):
            to = lax.rem(chan + i, NC)
            pltpu.make_async_remote_copy(
                src_ref=src.at[k, 0 if same else to, part],
                dst_ref=dst.at[k, chan, part],
                send_sem=ssem.at[phase, k],
                recv_sem=rsem.at[phase, k],
                device_id=(lat, to),
                device_id_type=MESH,
            ).start()
            return carry

        lax.fori_loop(1, NC, go, 0)

    def arrived(dst, phase, k, count, rows):
        part = dst.at[k, pl.ds(0, count), pl.ds(0, rows)]
        pltpu.make_async_copy(part, part, rsem.at[phase, k]).wait()

    def sent(dst, phase, k, count, rows):
        part = dst.at[k, pl.ds(0, count), pl.ds(0, rows)]
        pltpu.make_async_copy(part, part, ssem.at[phase, k]).wait()

    lane = lax.broadcasted_iota(jnp.int32, (BS, 128), 1)
    left = jnp.where(lane < TH, 1.0, 0.0).astype(BF16)
    right = jnp.where(lane >= TH, 1.0, 0.0).astype(BF16)
    own_lane = lax.rem(lanes(TH), TH) == lax.broadcasted_iota(jnp.int32, (TH, 128), 0)
    st_part[...] = jnp.zeros_like(st_part)
    for k in range(NCH):
        x_loads[k].wait()
        for r in range(NR):
            xr = x_ref[pl.ds((k * NR + r) * W, W), :]
            xf = xr.astype(F32)
            sq = xf * xf
            hi = sq.astype(BF16)
            lo = (sq - hi.astype(F32)).astype(BF16)
            sums = dot(xr, left) + dot(hi, right) + dot(lo, right)
            for j in range(TR):
                row = jnp.where(own_lane, sums[j * TH : (j + 1) * TH], 0.0)
                st_part[k, 0, pl.ds(r * TR + j, 1), :] = jnp.sum(row, axis=0, keepdims=True)
        if k == 0:
            pl.semaphore_wait(barrier, L - 1 + NC - 1)
        spread_chan(st_part, st_in, 0, k, 32, True)

    for c in s_loads:
        c.wait()
    nrm[...] = jnp.zeros_like(nrm)
    a_scr[pl.ds(NR * 96, 1024 - NR * 96), :] = jnp.zeros((1024 - NR * 96, 128), F32)
    for q in range(4):
        for b in range(2):
            blk = kept_lon[(q // 2) * 2 + b]
            fmat[pl.ds(q * 32 + b * 16, 16), :] = ftab[q % 2, blk]
    g = jnp.concatenate(
        [gtab[q % 2, kept_lon[(q // 2) * 2 + b]].astype(F32) for q in range(4) for b in range(2)],
        axis=0,
    )
    gmat[...] = g.T[0:W].astype(BF16)
    t = jnp.concatenate([ltab[q, kept_lat[b]].astype(F32) for q in range(2) for b in range(4)], axis=0)
    cs[...] = t.astype(BF16)
    ct[...] = t.T[0:H].astype(BF16)
    for src, dst in ((sw1, sf1), (sw2, sf2)):
        dst[...] = jnp.zeros_like(dst)
        real, imag = src[0], src[1]
        dst[pl.ds(0, BS), pl.ds(0, BS)] = real
        dst[pl.ds(0, BS), pl.ds(128, BS)] = imag
        dst[pl.ds(128, BS), pl.ds(0, BS)] = -imag
        dst[pl.ds(128, BS), pl.ds(128, BS)] = real

    def regroup(k, dst):
        for d in range(L):
            dst[k, d] = a_scr[pl.ds(d, 32, stride=32), :].astype(BF16)

    for k in range(NCH):
        arrived(st_in, 0, k, NC, 32)
        tot = st_in[k, 0]
        for i in range(1, NC):
            tot = tot + st_in[k, i]
        tot = tot * (1.0 / C)
        var = pltpu.roll(tot, TH, 1) - tot * tot
        scale = pltpu.roll(lax.rsqrt(var + EPS), TH, 1)
        stat = jnp.where(lanes(32) < TH, tot, scale).T
        for i in range(NR * TR):
            part = pl.ds(k * NR * W + i * TH, TH)
            xf = x_ref[part, :].astype(F32)
            normed = (xf - stat[0:TH, i : i + 1]) * stat[TH : 2 * TH, i : i + 1]
            nrm[part, pl.ds(0, BS)] = normed.astype(BF16)
        side = [nrm[pl.ds((k * NR + r) * W, W), :] for r in range(NR)]
        al = dot(fmat[...], jnp.concatenate(side, axis=1))
        for r in range(NR):
            parts = fold(*(al[q * 32 : (q + 1) * 32, r * 128 : (r + 1) * 128] for q in range(4)))
            for p in range(3):
                a_scr[pl.ds((r * 3 + p) * 32, 32), :] = parts[p]
        regroup(k, f_send)
        spread_lat(f_send, f_recv, 1, k)

    for k in range(NCH):
        arrived(f_recv, 1, k, L, 32)
        for s in range(L):
            r_scr[pl.ds(s * 32, 32), :] = f_recv[k, s].astype(F32)
        for n in range(SC):
            for hh in range(RH):
                for p in range(3):
                    row = (n * RH + hh) * 3 + p
                    b_scr[pl.ds(hh * 32, 32), pl.ds((n * 3 + p) * 128, 128)] = r_scr[
                        pl.ds(row, 32, stride=32), :
                    ].astype(BF16)
        both = dot(cs[:, 0:H], b_scr[...])
        for n in range(SC):
            cols = [slice((n * 3 + p) * 128, (n * 3 + p + 1) * 128) for p in range(3)]
            co = [both[0:64, c] for c in cols]
            si = [both[64:128, c] for c in cols]
            co.append(fourth(*co))
            si.append(fourth(*si))
            for m in range(2):
                rows = pl.ds((n * 2 + m) * 64, 64)
                sp[rows, pl.ds(0, 128)] = (co[2 * m] + si[2 * m + 1]).astype(BF16)
                sp[rows, pl.ds(128, 128)] = (co[2 * m + 1] - si[2 * m]).astype(BF16)
        one = jnp.maximum(dot(sp[...], sf1[...]), 0.0).astype(BF16)
        two = dot(one, sf2[...]).astype(BF16)
        side = []
        for i in range(SC * 2):
            f = two[i * 64 : (i + 1) * 64]
            turned = jnp.concatenate([-f[:, 128:256], f[:, 0:128]], axis=1)
            side.append(jnp.concatenate([f, turned], axis=0))
        wave = dot(ct[...], jnp.concatenate(side, axis=1))
        for n in range(SC):
            parts = fold(*(wave[:, (n * 4 + q) * 128 : (n * 4 + q + 1) * 128] for q in range(4)))
            for hh in range(RH):
                for p in range(3):
                    a_scr[pl.ds(((n * RH + hh) * 3 + p) * 32, 32), :] = parts[p][
                        hh * 32 : (hh + 1) * 32
                    ]
        regroup(k, b_send)
        spread_lat(b_send, b_recv, 2, k)

    for k in range(NCH):
        arrived(b_recv, 2, k, L, 32)
        for s in range(L):
            r_scr[pl.ds(s * 32, 32), :] = b_recv[k, s].astype(F32)
        side = []
        for r in range(NR):
            parts = [r_scr[pl.ds(r * 3 + p, 32, stride=32), :] for p in range(3)]
            side.append(jnp.concatenate(parts + [fourth(*parts)], axis=0).astype(BF16))
        spectral = dot(gmat[...], jnp.concatenate(side, axis=1))
        for r in range(NR):
            at = pl.ds((k * NR + r) * W, W)
            mixed = x_ref[at, :].astype(F32) + nrm[at, pl.ds(0, BS)].astype(F32)
            mixed = mixed + spectral[:, r * 128 : r * 128 + BS]
            g = k * NR + r
            j = sum(g >= v for v in BOUNDS[1:])
            for d in range(NC):
                m_scr[d, pl.ds(g * WS, WS), pl.ds(0, BS)] = mixed[d * WS : (d + 1) * WS]
            if g == BOUNDS[j + 1] - 1:
                for d in range(NC):
                    c_send[j, d, pl.ds(0, PACKED[j]), :] = fold_cells(
                        m_scr[d, pl.ds(BOUNDS[j] * WS, ROWS[j] * WS), :], CUTS[ROWS[j]]
                    )
                spread_chan(c_send, c_recv, 3, j, PACKED[j], False)

    for c in loads:
        c.wait()
    for k in range(NT):
        arrived(c_recv, 3, k, NC, PACKED[k])
        cuts = CUTS[ROWS[k]]
        cells = ROWS[k] * WS
        lane = lanes(cells)
        acc = jnp.zeros((cells, 128), F32)
        acc2 = jnp.zeros((cells, 128), F32)
        for s in range(NC):
            y = unfold_cells(c_recv[k, s, pl.ds(0, PACKED[k]), :], cuts)
            y = jnp.where(lane < BS, y, 0.0)
            y_scr[s, pl.ds(0, cells), :] = y
            acc = acc + y
            acc2 = acc2 + y * y
        mean = jnp.sum(acc, axis=1, keepdims=True) * (1.0 / C)
        var = jnp.sum(acc2, axis=1, keepdims=True) * (1.0 / C) - mean * mean
        scale = lax.rsqrt(var + EPS)
        for i in range(2):
            z = [(y_scr[4 * i + j, pl.ds(0, cells), :] - mean) * scale for j in range(4)]
            z = [z[0]] + [pltpu.roll(z[j], 128 - 32 * j, 1) for j in range(1, 4)]
            for j in range(3):
                tile = jnp.where(lane < BS - 32 * j, z[j], z[j + 1])
                n2[pl.ds(0, cells), pl.ds((3 * i + j) * 128, 128)] = tile.astype(BF16)
        n2k = n2[pl.ds(0, cells), :]
        for i in range(HID // 512):
            cols = pl.ds(i * 512, 512)
            hid[pl.ds(0, cells), cols] = gelu(dot(n2k, w1v[:, cols])).astype(BF16)
        o = dot(hid[pl.ds(0, cells), :], w2v[...])
        tiles = [o[:, i * 128 : (i + 1) * 128] for i in range(6)]
        for s in range(NC):
            i, off = divmod(s * BS, 128)
            piece = tiles[i]
            if off:
                piece = pltpu.roll(piece, 128 - off, 1)
                if off > 32:
                    after = pltpu.roll(tiles[i + 1], 128 - off, 1)
                    piece = jnp.where(lane < 128 - off, piece, after)
            d_send[k, s, pl.ds(0, PACKED[k]), :] = fold_cells(
                y_scr[s, pl.ds(0, cells), :] + piece, cuts
            )
        spread_chan(d_send, d_recv, 4, k, PACKED[k], False)

    stores = []
    for k in range(NT):
        arrived(d_recv, 4, k, NC, PACKED[k])
        for s in range(NC):
            y = unfold_cells(d_recv[k, s, pl.ds(0, PACKED[k]), :], CUTS[ROWS[k]])
            for r in range(ROWS[k]):
                o_scr[pl.ds(r * W + s * WS, WS), :] = y[r * WS : (r + 1) * WS]
        at = pl.ds(BOUNDS[k] * W, ROWS[k] * W)
        o_buf[at, :] = o_scr[pl.ds(0, ROWS[k] * W), 0:BS].astype(BF16)
        stores.append(pltpu.make_async_copy(o_buf.at[at], out_hbm.at[at], osem.at[k]))
        stores[k].start()
    for c in stores:
        c.wait()
    for k in range(NCH):
        sent(st_in, 0, k, NC - 1, 32)
        sent(f_send, 1, k, L - 1, 32)
        sent(b_send, 2, k, L - 1, 32)
    for k in range(NT):
        sent(c_send, 3, k, NC - 1, PACKED[k])
        sent(d_send, 4, k, NC - 1, PACKED[k])


def hand_on(i_ref, o_ref, buf, sem_in, sem_out):
    step = i_ref.shape[0] // 6
    parts = [pl.ds(i * step, step) for i in range(6)]
    reads = [pltpu.make_async_copy(i_ref.at[p], buf.at[p], sem_in.at[i]) for i, p in enumerate(parts)]
    writes = [pltpu.make_async_copy(buf.at[p], o_ref.at[p], sem_out.at[i]) for i, p in enumerate(parts)]
    for c in reads:
        c.start()
    for r, w in zip(reads, writes):
        r.wait()
        w.start()
    for c in writes:
        c.wait()


def on_device(fields, kept_lat, kept_lon, spec_w1, spec_w2, mlp_w1, mlp_w2):
    fwd, inv, lat = tables()
    hbm = pl.BlockSpec(memory_space=pltpu.HBM)
    cells = S * RH * W
    parts = pl.pallas_call(
        kernel,
        out_shape=jax.ShapeDtypeStruct((cells, BS), BF16),
        in_specs=[hbm] * 10,
        out_specs=hbm,
        scratch_shapes=[
            pltpu.SMEM((4,), jnp.int32),
            pltpu.SMEM((4,), jnp.int32),
            pltpu.VMEM((cells, BS), BF16),
            pltpu.VMEM((2, BS, BS), BF16),
            pltpu.VMEM((2, BS, BS), BF16),
            pltpu.VMEM(fwd.shape, BF16),
            pltpu.VMEM(inv.shape, BF16),
            pltpu.VMEM(lat.shape, BF16),
            pltpu.VMEM((128, W), BF16),
            pltpu.VMEM((W, 128), BF16),
            pltpu.VMEM((128, 128), BF16),
            pltpu.VMEM((H, 128), BF16),
            pltpu.VMEM((256, 256), BF16),
            pltpu.VMEM((256, 256), BF16),
            pltpu.VMEM((C, HID), BF16),
            pltpu.VMEM((HID, C), BF16),
            pltpu.VMEM((NCH, 1, 32, 128), F32),
            pltpu.VMEM((NCH, NC, 32, 128), F32),
            pltpu.VMEM((cells, 128), BF16),
            pltpu.VMEM((1024, 128), F32),
            pltpu.VMEM((NCH, L, 32, 128), BF16),
            pltpu.VMEM((NCH, L, 32, 128), BF16),
            pltpu.VMEM((1024, 128), F32),
            pltpu.VMEM((H, SC * 384), BF16),
            pltpu.VMEM((SC * 128, 256), BF16),
            pltpu.VMEM((NCH, L, 32, 128), BF16),
            pltpu.VMEM((NCH, L, 32, 128), BF16),
            pltpu.VMEM((NC, S * RH * WS, 128), F32),
            pltpu.VMEM((NT, NC, MAXP, 128), BF16),
            pltpu.VMEM((NT, NC, MAXP, 128), BF16),
            pltpu.VMEM((NC, MAXC, 128), F32),
            pltpu.VMEM((MAXC, C), BF16),
            pltpu.VMEM((MAXC, HID), BF16),
            pltpu.VMEM((NT, NC, MAXP, 128), BF16),
            pltpu.VMEM((NT, NC, MAXP, 128), BF16),
            pltpu.VMEM((max(ROWS) * W, 128), F32),
            pltpu.VMEM((cells, BS), BF16),
            pltpu.SemaphoreType.DMA((2,)),
            pltpu.SemaphoreType.DMA((NCH + 7,)),
            pltpu.SemaphoreType.DMA((NT,)),
            pltpu.SemaphoreType.DMA((5, NT)),
            pltpu.SemaphoreType.DMA((5, NT)),
        ],
        compiler_params=pltpu.CompilerParams(
            collective_id=0, has_side_effects=True, vmem_limit_bytes=56 * 1024 * 1024
        ),
        cost_estimate=pl.CostEstimate(
            flops=5_000_000_000, bytes_accessed=12_000_000, transcendentals=1_400_000
        ),
    )(
        kept_lat,
        kept_lon,
        fields.reshape(cells, BS),
        spec_w1.reshape(2, BS, BS),
        spec_w2.reshape(2, BS, BS),
        fwd,
        inv,
        lat,
        mlp_w1,
        mlp_w2,
    )
    out = pl.pallas_call(
        hand_on,
        out_shape=jax.ShapeDtypeStruct((cells, BS), BF16),
        in_specs=[pl.BlockSpec(memory_space=pltpu.HBM)],
        out_specs=pl.BlockSpec(memory_space=pltpu.HBM),
        scratch_shapes=[
            pltpu.VMEM((cells, BS), BF16),
            pltpu.SemaphoreType.DMA((6,)),
            pltpu.SemaphoreType.DMA((6,)),
        ],
    )(parts)
    return out.reshape(S, RH, W, BS)


def solution(mesh):
    placed = (
        P(None, "lat", None, "chan"),
        P(),
        P(),
        P(None, "chan", None, None),
        P(None, "chan", None, None),
        P(),
        P(),
    )
    return jax.shard_map(
        on_device,
        mesh=mesh,
        in_specs=placed,
        out_specs=P(None, "lat", None, "chan"),
        check_vma=False,
    )
```

```python
import math

import jax
import jax.numpy as jnp
import numpy as np
from jax import lax
from jax.experimental import pallas as pl
from jax.experimental.pallas import tpu as pltpu
from jax.sharding import PartitionSpec as P

S, H, W, C, HID, BS = 6, 96, 192, 768, 3072, 96
L, NC = 32, 8
RH = H // L
NCH = 2
SC = S // NCH
NG = S * RH
NB = 7
OUT_PAIRS, OUT_BLOCKS = (0, 11, 18), (0, 4, 7)
BACK_PAIRS, BACK_BLOCKS = (0, 8, 18), (0, 3, 7)
WS = W // NC
BOUNDS = (0, 8, 14, 18)
NT = len(BOUNDS) - 1
CUTS = {
    8: (0, 48, 96, 144, 192),
    6: (0, 40, 80, 112, 144),
    4: (0, 32, 56, 80, 96),
}
ROWS = [BOUNDS[j + 1] - BOUNDS[j] for j in range(NT)]
PACKED = [CUTS[n][3] for n in ROWS]
MAXC, MAXP = max(ROWS) * WS, max(PACKED)
TH = 64
TR = W // TH
STAT_ROWS = (40, 24)
EPS = 1e-5
F32, BF16 = jnp.float32, jnp.bfloat16
MESH = pl.DeviceIdType.MESH


def tables():
    k = np.arange(96)
    w = np.arange(W)
    angle = 2.0 * np.pi / W * ((k[:, None] * w[None, :]) % W)
    fwd = np.stack([np.cos(angle), -np.sin(angle)]) / math.sqrt(W)
    gain = np.where(k > 0, 2.0, 1.0)[:, None] / math.sqrt(W)
    inv = np.zeros((2, 96, 256))
    inv[:, :, :W] = np.stack([np.cos(angle) * gain, -np.sin(angle) * gain])
    h = (np.arange(L)[None, :] * RH + np.arange(RH)[:, None]).reshape(-1)
    angle = 2.0 * np.pi / H * ((k[:, None] * h[None, :]) % H)
    lat = np.zeros((2, 96, 128))
    lat[:, :, :H] = np.stack([np.cos(angle), np.sin(angle)]) / math.sqrt(H)
    cast = lambda t: jnp.asarray(t.reshape(2, 6, 16, -1).astype(np.float32), dtype=BF16)
    return cast(fwd), cast(inv), cast(lat)


def lanes(rows):
    return lax.broadcasted_iota(jnp.int32, (rows, 128), 1)


def fold(a0, a1, a2, a3):
    low = lanes(a0.shape[0]) < BS
    return (
        jnp.where(low, a0, pltpu.roll(a3, 96, 1)),
        jnp.where(low, a1, pltpu.roll(a3, 64, 1)),
        jnp.where(low, a2, pltpu.roll(a3, 32, 1)),
    )


def fourth(t0, t1, t2):
    lane = lanes(t0.shape[0])
    return jnp.where(
        lane < 32,
        pltpu.roll(t0, 32, 1),
        jnp.where(lane < 64, pltpu.roll(t1, 64, 1), pltpu.roll(t2, 96, 1)),
    )


def dot(a, b):
    return jnp.dot(a, b, preferred_element_type=F32)


def fold_cells(m, cuts):
    last = m[cuts[3] : cuts[4]]
    out = []
    for g in range(3):
        here = m[cuts[g] : cuts[g + 1]]
        extra = here.shape[0] - last.shape[0]
        add = jnp.concatenate([last, jnp.zeros((extra, 128), F32)], axis=0) if extra else last
        out.append(jnp.where(lanes(here.shape[0]) < BS, here, pltpu.roll(add, 96 - 32 * g, 1)))
    return jnp.concatenate(out, axis=0).astype(BF16)


def unfold_cells(t, cuts):
    t = t.astype(F32)
    parts = [t[cuts[g] : cuts[g + 1]] for g in range(3)]
    n = cuts[4] - cuts[3]
    return jnp.concatenate(parts + [fourth(*(p[0:n] for p in parts))], axis=0)


def gelu(u):
    return 0.5 * u * (1.0 + lax.erf(u * (1.0 / math.sqrt(2.0))))


def kernel(
    lat_hbm,
    lon_hbm,
    x_hbm,
    sw1_hbm,
    sw2_hbm,
    ftab_hbm,
    gtab_hbm,
    ltab_hbm,
    w1_hbm,
    w2_hbm,
    out_hbm,
    kept_lat,
    kept_lon,
    x_ref,
    sw1,
    sw2,
    ftab,
    gtab,
    ltab,
    fmat,
    gmat,
    cs,
    ct,
    sf1,
    sf2,
    w1v,
    w2v,
    st_part,
    st_in,
    nrm,
    a_scr,
    f_send,
    f_recv,
    r_scr,
    b_scr,
    sp,
    b_send,
    b_recv,
    m_scr,
    c_send,
    c_recv,
    y_scr,
    n2,
    hid,
    d_send,
    d_recv,
    o_scr,
    o_buf,
    wsem,
    isem,
    osem,
    ssem,
    rsem,
):
    lat = lax.axis_index("lat")
    chan = lax.axis_index("chan")

    x_parts = [
        pl.ds(OUT_PAIRS[k] * W, (OUT_PAIRS[k + 1] - OUT_PAIRS[k]) * W) for k in range(NCH)
    ]
    x_loads = [
        pltpu.make_async_copy(x_hbm.at[part], x_ref.at[part], isem.at[k])
        for k, part in enumerate(x_parts)
    ]
    small = (
        (lat_hbm, kept_lat),
        (lon_hbm, kept_lon),
        (ftab_hbm, ftab),
        (gtab_hbm, gtab),
        (ltab_hbm, ltab),
        (sw1_hbm, sw1),
        (sw2_hbm, sw2),
    )
    s_loads = [
        pltpu.make_async_copy(src, dst, isem.at[NCH + i]) for i, (src, dst) in enumerate(small)
    ]
    loads = [
        pltpu.make_async_copy(w1_hbm, w1v, wsem.at[0]),
        pltpu.make_async_copy(w2_hbm, w2v, wsem.at[1]),
    ]
    for c in x_loads:
        c.start()

    barrier = pltpu.get_barrier_semaphore()

    def greet_lat(i, carry):
        pl.semaphore_signal(
            barrier, inc=1, device_id=(lax.rem(lat + i, L), chan), device_id_type=MESH
        )
        return carry

    def greet_chan(i, carry):
        pl.semaphore_signal(
            barrier, inc=1, device_id=(lat, lax.rem(chan + i, NC)), device_id_type=MESH
        )
        return carry

    lax.fori_loop(1, L, greet_lat, 0)
    lax.fori_loop(1, NC, greet_chan, 0)
    for c in s_loads + loads:
        c.start()

    def spread_lat(src, dst, phase, k, bounds):
        part = pl.ds(bounds[k], bounds[k + 1] - bounds[k])
        pltpu.make_async_copy(src.at[lat, part], dst.at[lat, part], rsem.at[phase, k]).start()

        def go(i, carry):
            to = lax.rem(lat + i, L)
            pltpu.make_async_remote_copy(
                src_ref=src.at[to, part],
                dst_ref=dst.at[lat, part],
                send_sem=ssem.at[phase, k],
                recv_sem=rsem.at[phase, k],
                device_id=(to, chan),
                device_id_type=MESH,
            ).start()
            return carry

        lax.fori_loop(1, L, go, 0)

    def arrived_lat(dst, phase, k, bounds):
        part = dst.at[pl.ds(0, L), pl.ds(bounds[k], bounds[k + 1] - bounds[k])]
        pltpu.make_async_copy(part, part, rsem.at[phase, k]).wait()
        for s in range(L):
            for b in range(bounds[k], bounds[k + 1]):
                r_scr[pl.ds((s * NB + b) * 8, 8), :] = dst[s, b].astype(F32)

    def sent_lat(dst, phase, k, bounds):
        part = dst.at[pl.ds(0, L - 1), pl.ds(bounds[k], bounds[k + 1] - bounds[k])]
        pltpu.make_async_copy(part, part, ssem.at[phase, k]).wait()

    def regroup(dst, k, bounds):
        for d in range(L):
            for b in range(bounds[k], bounds[k + 1]):
                dst[d, b] = a_scr[pl.ds(b * 256 + d, 8, stride=32), :].astype(BF16)

    def spread_chan(src, dst, phase, k, rows, same):
        part = pl.ds(0, rows)
        own = src.at[k, 0 if same else chan, part]
        pltpu.make_async_copy(own, dst.at[k, chan, part], rsem.at[phase, k]).start()

        def go(i, carry):
            to = lax.rem(chan + i, NC)
            pltpu.make_async_remote_copy(
                src_ref=src.at[k, 0 if same else to, part],
                dst_ref=dst.at[k, chan, part],
                send_sem=ssem.at[phase, k],
                recv_sem=rsem.at[phase, k],
                device_id=(lat, to),
                device_id_type=MESH,
            ).start()
            return carry

        lax.fori_loop(1, NC, go, 0)

    def arrived(dst, phase, k, count, rows):
        part = dst.at[k, pl.ds(0, count), pl.ds(0, rows)]
        pltpu.make_async_copy(part, part, rsem.at[phase, k]).wait()

    def sent(dst, phase, k, count, rows):
        part = dst.at[k, pl.ds(0, count), pl.ds(0, rows)]
        pltpu.make_async_copy(part, part, ssem.at[phase, k]).wait()

    lane = lax.broadcasted_iota(jnp.int32, (BS, 128), 1)
    left = jnp.where(lane < TH, 1.0, 0.0).astype(BF16)
    right = jnp.where(lane >= TH, 1.0, 0.0).astype(BF16)
    own_lane = lax.rem(lanes(TH), TH) == lax.broadcasted_iota(jnp.int32, (TH, 128), 0)
    st_part[...] = jnp.zeros_like(st_part)
    for k in range(NCH):
        x_loads[k].wait()
        for g in range(OUT_PAIRS[k], OUT_PAIRS[k + 1]):
            xr = x_ref[pl.ds(g * W, W), :]
            xf = xr.astype(F32)
            sq = xf * xf
            hi = sq.astype(BF16)
            lo = (sq - hi.astype(F32)).astype(BF16)
            sums = dot(xr, left) + dot(hi, right) + dot(lo, right)
            for j in range(TR):
                row = jnp.where(own_lane, sums[j * TH : (j + 1) * TH], 0.0)
                st_part[k, 0, pl.ds((g - OUT_PAIRS[k]) * TR + j, 1), :] = jnp.sum(row, axis=0, keepdims=True)
        if k == 0:
            pl.semaphore_wait(barrier, L - 1 + NC - 1)
        spread_chan(st_part, st_in, 0, k, STAT_ROWS[k], True)

    for c in s_loads:
        c.wait()
    nrm[...] = jnp.zeros_like(nrm)
    a_scr[pl.ds(NG * 96, 64), :] = jnp.zeros((64, 128), F32)
    for q in range(4):
        for b in range(2):
            blk = kept_lon[(q // 2) * 2 + b]
            fmat[pl.ds(q * 32 + b * 16, 16), :] = ftab[q % 2, blk]
    g = jnp.concatenate(
        [gtab[q % 2, kept_lon[(q // 2) * 2 + b]].astype(F32) for q in range(4) for b in range(2)],
        axis=0,
    )
    gmat[...] = g.T[0:W].astype(BF16)
    t = jnp.concatenate([ltab[q, kept_lat[b]].astype(F32) for q in range(2) for b in range(4)], axis=0)
    cs[...] = t.astype(BF16)
    ct[...] = t.T[0:H].astype(BF16)
    for src, dst in ((sw1, sf1), (sw2, sf2)):
        dst[...] = jnp.zeros_like(dst)
        real, imag = src[0], src[1]
        dst[pl.ds(0, BS), pl.ds(0, BS)] = real
        dst[pl.ds(0, BS), pl.ds(128, BS)] = imag
        dst[pl.ds(128, BS), pl.ds(0, BS)] = -imag
        dst[pl.ds(128, BS), pl.ds(128, BS)] = real

    for k in range(NCH):
        arrived(st_in, 0, k, NC, STAT_ROWS[k])
        rows = pl.ds(0, STAT_ROWS[k])
        tot = st_in[k, 0, rows, :]
        for i in range(1, NC):
            tot = tot + st_in[k, i, rows, :]
        tot = tot * (1.0 / C)
        var = pltpu.roll(tot, TH, 1) - tot * tot
        scale = pltpu.roll(lax.rsqrt(var + EPS), TH, 1)
        stat = jnp.where(lanes(STAT_ROWS[k]) < TH, tot, scale).T
        pairs = range(OUT_PAIRS[k], OUT_PAIRS[k + 1])
        for i in range(len(pairs) * TR):
            part = pl.ds(pairs[0] * W + i * TH, TH)
            xf = x_ref[part, :].astype(F32)
            normed = (xf - stat[0:TH, i : i + 1]) * stat[TH : 2 * TH, i : i + 1]
            nrm[part, pl.ds(0, BS)] = normed.astype(BF16)
        side = [nrm[pl.ds(g * W, W), :] for g in pairs]
        al = dot(fmat[...], jnp.concatenate(side, axis=1))
        for r, g in enumerate(pairs):
            parts = fold(*(al[q * 32 : (q + 1) * 32, r * 128 : (r + 1) * 128] for q in range(4)))
            for p in range(3):
                a_scr[pl.ds((g * 3 + p) * 32, 32), :] = parts[p]
        regroup(f_send, k, OUT_BLOCKS)
        spread_lat(f_send, f_recv, 1, k, OUT_BLOCKS)

    for k in range(NCH):
        arrived_lat(f_recv, 1, k, OUT_BLOCKS)
        for n in range(SC):
            for hh in range(RH):
                for p in range(3):
                    row = ((k * SC + n) * RH + hh) * 3 + p
                    b_scr[pl.ds(hh * 32, 32), pl.ds((n * 3 + p) * 128, 128)] = r_scr[
                        pl.ds(row, 32, stride=NB * 8), :
                    ].astype(BF16)
        both = dot(cs[:, 0:H], b_scr[...])
        for n in range(SC):
            cols = [slice((n * 3 + p) * 128, (n * 3 + p + 1) * 128) for p in range(3)]
            co = [both[0:64, c] for c in cols]
            si = [both[64:128, c] for c in cols]
            co.append(fourth(*co))
            si.append(fourth(*si))
            for m in range(2):
                rows = pl.ds((n * 2 + m) * 64, 64)
                sp[rows, pl.ds(0, 128)] = (co[2 * m] + si[2 * m + 1]).astype(BF16)
                sp[rows, pl.ds(128, 128)] = (co[2 * m + 1] - si[2 * m]).astype(BF16)
        one = jnp.maximum(dot(sp[...], sf1[...]), 0.0).astype(BF16)
        two = dot(one, sf2[...]).astype(BF16)
        side = []
        for i in range(SC * 2):
            f = two[i * 64 : (i + 1) * 64]
            turned = jnp.concatenate([-f[:, 128:256], f[:, 0:128]], axis=1)
            side.append(jnp.concatenate([f, turned], axis=0))
        wave = dot(ct[...], jnp.concatenate(side, axis=1))
        for n in range(SC):
            parts = fold(*(wave[:, (n * 4 + q) * 128 : (n * 4 + q + 1) * 128] for q in range(4)))
            for hh in range(RH):
                for p in range(3):
                    row = ((k * SC + n) * RH + hh) * 3 + p
                    a_scr[pl.ds(row * 32, 32), :] = parts[p][hh * 32 : (hh + 1) * 32]
        regroup(b_send, k, BACK_BLOCKS)
        spread_lat(b_send, b_recv, 2, k, BACK_BLOCKS)

    for k in range(NCH):
        arrived_lat(b_recv, 2, k, BACK_BLOCKS)
        pairs = range(BACK_PAIRS[k], BACK_PAIRS[k + 1])
        side = []
        for g in pairs:
            parts = [r_scr[pl.ds(g * 3 + p, 32, stride=NB * 8), :] for p in range(3)]
            side.append(jnp.concatenate(parts + [fourth(*parts)], axis=0).astype(BF16))
        spectral = dot(gmat[...], jnp.concatenate(side, axis=1))
        for r, g in enumerate(pairs):
            at = pl.ds(g * W, W)
            mixed = x_ref[at, :].astype(F32) + nrm[at, pl.ds(0, BS)].astype(F32)
            mixed = mixed + spectral[:, r * 128 : r * 128 + BS]
            j = sum(g >= v for v in BOUNDS[1:])
            for d in range(NC):
                m_scr[d, pl.ds(g * WS, WS), pl.ds(0, BS)] = mixed[d * WS : (d + 1) * WS]
            if g == BOUNDS[j + 1] - 1:
                for d in range(NC):
                    c_send[j, d, pl.ds(0, PACKED[j]), :] = fold_cells(
                        m_scr[d, pl.ds(BOUNDS[j] * WS, ROWS[j] * WS), :], CUTS[ROWS[j]]
                    )
                spread_chan(c_send, c_recv, 3, j, PACKED[j], False)

    for c in loads:
        c.wait()
    for k in range(NT):
        arrived(c_recv, 3, k, NC, PACKED[k])
        cuts = CUTS[ROWS[k]]
        cells = ROWS[k] * WS
        lane = lanes(cells)
        acc = jnp.zeros((cells, 128), F32)
        acc2 = jnp.zeros((cells, 128), F32)
        for s in range(NC):
            y = unfold_cells(c_recv[k, s, pl.ds(0, PACKED[k]), :], cuts)
            y = jnp.where(lane < BS, y, 0.0)
            y_scr[s, pl.ds(0, cells), :] = y
            acc = acc + y
            acc2 = acc2 + y * y
        mean = jnp.sum(acc, axis=1, keepdims=True) * (1.0 / C)
        var = jnp.sum(acc2, axis=1, keepdims=True) * (1.0 / C) - mean * mean
        scale = lax.rsqrt(var + EPS)
        for i in range(2):
            z = [(y_scr[4 * i + j, pl.ds(0, cells), :] - mean) * scale for j in range(4)]
            z = [z[0]] + [pltpu.roll(z[j], 128 - 32 * j, 1) for j in range(1, 4)]
            for j in range(3):
                tile = jnp.where(lane < BS - 32 * j, z[j], z[j + 1])
                n2[pl.ds(0, cells), pl.ds((3 * i + j) * 128, 128)] = tile.astype(BF16)
        n2k = n2[pl.ds(0, cells), :]
        for i in range(HID // 512):
            cols = pl.ds(i * 512, 512)
            hid[pl.ds(0, cells), cols] = gelu(dot(n2k, w1v[:, cols])).astype(BF16)
        o = dot(hid[pl.ds(0, cells), :], w2v[...])
        tiles = [o[:, i * 128 : (i + 1) * 128] for i in range(6)]
        for s in range(NC):
            i, off = divmod(s * BS, 128)
            piece = tiles[i]
            if off:
                piece = pltpu.roll(piece, 128 - off, 1)
                if off > 32:
                    after = pltpu.roll(tiles[i + 1], 128 - off, 1)
                    piece = jnp.where(lane < 128 - off, piece, after)
            d_send[k, s, pl.ds(0, PACKED[k]), :] = fold_cells(
                y_scr[s, pl.ds(0, cells), :] + piece, cuts
            )
        spread_chan(d_send, d_recv, 4, k, PACKED[k], False)

    stores = []
    for k in range(NT):
        arrived(d_recv, 4, k, NC, PACKED[k])
        for s in range(NC):
            y = unfold_cells(d_recv[k, s, pl.ds(0, PACKED[k]), :], CUTS[ROWS[k]])
            for r in range(ROWS[k]):
                o_scr[pl.ds(r * W + s * WS, WS), :] = y[r * WS : (r + 1) * WS]
        at = pl.ds(BOUNDS[k] * W, ROWS[k] * W)
        o_buf[at, :] = o_scr[pl.ds(0, ROWS[k] * W), :].astype(BF16)
        stores.append(pltpu.make_async_copy(o_buf.at[at], out_hbm.at[at], osem.at[k]))
        stores[k].start()
    for c in stores:
        c.wait()
    for k in range(NCH):
        sent(st_in, 0, k, NC - 1, STAT_ROWS[k])
        sent_lat(f_send, 1, k, OUT_BLOCKS)
        sent_lat(b_send, 2, k, BACK_BLOCKS)
    for k in range(NT):
        sent(c_send, 3, k, NC - 1, PACKED[k])
        sent(d_send, 4, k, NC - 1, PACKED[k])


def hand_on(i_ref, o_ref, buf, narrow, sem_in, sem_out):
    step = i_ref.shape[0] // 6
    parts = [pl.ds(i * step, step) for i in range(6)]
    reads = [pltpu.make_async_copy(i_ref.at[p], buf.at[p], sem_in.at[i]) for i, p in enumerate(parts)]
    writes = [pltpu.make_async_copy(narrow.at[p], o_ref.at[p], sem_out.at[i]) for i, p in enumerate(parts)]
    for c in reads:
        c.start()
    for p, r, w in zip(parts, reads, writes):
        r.wait()
        narrow[p, :] = buf[p, 0:BS]
        w.start()
    for c in writes:
        c.wait()


def on_device(fields, kept_lat, kept_lon, spec_w1, spec_w2, mlp_w1, mlp_w2):
    fwd, inv, lat = tables()
    hbm = pl.BlockSpec(memory_space=pltpu.HBM)
    cells = S * RH * W
    parts = pl.pallas_call(
        kernel,
        out_shape=jax.ShapeDtypeStruct((cells, 128), BF16),
        in_specs=[hbm] * 10,
        out_specs=hbm,
        scratch_shapes=[
            pltpu.SMEM((4,), jnp.int32),
            pltpu.SMEM((4,), jnp.int32),
            pltpu.VMEM((cells, BS), BF16),
            pltpu.VMEM((2, BS, BS), BF16),
            pltpu.VMEM((2, BS, BS), BF16),
            pltpu.VMEM(fwd.shape, BF16),
            pltpu.VMEM(inv.shape, BF16),
            pltpu.VMEM(lat.shape, BF16),
            pltpu.VMEM((128, W), BF16),
            pltpu.VMEM((W, 128), BF16),
            pltpu.VMEM((128, 128), BF16),
            pltpu.VMEM((H, 128), BF16),
            pltpu.VMEM((256, 256), BF16),
            pltpu.VMEM((256, 256), BF16),
            pltpu.VMEM((C, HID), BF16),
            pltpu.VMEM((HID, C), BF16),
            pltpu.VMEM((NCH, 1, STAT_ROWS[0], 128), F32),
            pltpu.VMEM((NCH, NC, STAT_ROWS[0], 128), F32),
            pltpu.VMEM((cells, 128), BF16),
            pltpu.VMEM((NB * 256, 128), F32),
            pltpu.VMEM((L, NB, 8, 128), BF16),
            pltpu.VMEM((L, NB, 8, 128), BF16),
            pltpu.VMEM((NB * 256, 128), F32),
            pltpu.VMEM((H, SC * 384), BF16),
            pltpu.VMEM((SC * 128, 256), BF16),
            pltpu.VMEM((L, NB, 8, 128), BF16),
            pltpu.VMEM((L, NB, 8, 128), BF16),
            pltpu.VMEM((NC, S * RH * WS, 128), F32),
            pltpu.VMEM((NT, NC, MAXP, 128), BF16),
            pltpu.VMEM((NT, NC, MAXP, 128), BF16),
            pltpu.VMEM((NC, MAXC, 128), F32),
            pltpu.VMEM((MAXC, C), BF16),
            pltpu.VMEM((MAXC, HID), BF16),
            pltpu.VMEM((NT, NC, MAXP, 128), BF16),
            pltpu.VMEM((NT, NC, MAXP, 128), BF16),
            pltpu.VMEM((max(ROWS) * W, 128), F32),
            pltpu.VMEM((cells, 128), BF16),
            pltpu.SemaphoreType.DMA((2,)),
            pltpu.SemaphoreType.DMA((NCH + 7,)),
            pltpu.SemaphoreType.DMA((NT,)),
            pltpu.SemaphoreType.DMA((5, NT)),
            pltpu.SemaphoreType.DMA((5, NT)),
        ],
        compiler_params=pltpu.CompilerParams(
            collective_id=0, has_side_effects=True, vmem_limit_bytes=56 * 1024 * 1024
        ),
        cost_estimate=pl.CostEstimate(
            flops=5_000_000_000, bytes_accessed=12_000_000, transcendentals=1_400_000
        ),
    )(
        kept_lat,
        kept_lon,
        fields.reshape(cells, BS),
        spec_w1.reshape(2, BS, BS),
        spec_w2.reshape(2, BS, BS),
        fwd,
        inv,
        lat,
        mlp_w1,
        mlp_w2,
    )
    out = pl.pallas_call(
        hand_on,
        out_shape=jax.ShapeDtypeStruct((cells, BS), BF16),
        in_specs=[pl.BlockSpec(memory_space=pltpu.HBM)],
        out_specs=pl.BlockSpec(memory_space=pltpu.HBM),
        scratch_shapes=[
            pltpu.VMEM((cells, 128), BF16),
            pltpu.VMEM((cells, BS), BF16),
            pltpu.SemaphoreType.DMA((6,)),
            pltpu.SemaphoreType.DMA((6,)),
        ],
    )(parts)
    return out.reshape(S, RH, W, BS)


def solution(mesh):
    placed = (
        P(None, "lat", None, "chan"),
        P(),
        P(),
        P(None, "chan", None, None),
        P(None, "chan", None, None),
        P(),
        P(),
    )
    return jax.shard_map(
        on_device,
        mesh=mesh,
        in_specs=placed,
        out_specs=P(None, "lat", None, "chan"),
        check_vma=False,
    )
```

```python
import math

import jax
import jax.numpy as jnp
import numpy as np
from jax import lax
from jax.experimental import pallas as pl
from jax.experimental.pallas import tpu as pltpu
from jax.sharding import PartitionSpec as P

S, H, W, C, HID, BS = 6, 96, 192, 768, 3072, 96
L, NC = 32, 8
RH = H // L
NCH = 2
SC = S // NCH
NG = S * RH
NB = 7
OUT_PAIRS, OUT_BLOCKS = (0, 11, 18), (0, 4, 7)
BACK_PAIRS, BACK_BLOCKS = (0, 8, 18), (0, 3, 7)
WS = W // NC
BOUNDS = (0, 8, 13, 18)
NT = len(BOUNDS) - 1
CUTS = {
    8: (0, 48, 96, 144, 192),
    6: (0, 40, 80, 112, 144),
    5: (0, 32, 64, 96, 120),
    4: (0, 32, 56, 80, 96),
}
ROWS = [BOUNDS[j + 1] - BOUNDS[j] for j in range(NT)]
PACKED = [CUTS[n][3] for n in ROWS]
MAXC, MAXP = max(ROWS) * WS, max(PACKED)
TH = 64
TR = W // TH
STAT_ROWS = (40, 24)
EPS = 1e-5
F32, BF16 = jnp.float32, jnp.bfloat16
MESH = pl.DeviceIdType.MESH


def tables():
    k = np.arange(96)
    w = np.arange(W)
    angle = 2.0 * np.pi / W * ((k[:, None] * w[None, :]) % W)
    fwd = np.stack([np.cos(angle), -np.sin(angle)]) / math.sqrt(W)
    gain = np.where(k > 0, 2.0, 1.0)[:, None] / math.sqrt(W)
    inv = np.zeros((2, 96, 256))
    inv[:, :, :W] = np.stack([np.cos(angle) * gain, -np.sin(angle) * gain])
    h = (np.arange(L)[None, :] * RH + np.arange(RH)[:, None]).reshape(-1)
    angle = 2.0 * np.pi / H * ((k[:, None] * h[None, :]) % H)
    lat = np.zeros((2, 96, 128))
    lat[:, :, :H] = np.stack([np.cos(angle), np.sin(angle)]) / math.sqrt(H)
    cast = lambda t: jnp.asarray(t.reshape(2, 6, 16, -1).astype(np.float32), dtype=BF16)
    return cast(fwd), cast(inv), cast(lat)


def lanes(rows):
    return lax.broadcasted_iota(jnp.int32, (rows, 128), 1)


def fold(a0, a1, a2, a3):
    low = lanes(a0.shape[0]) < BS
    return (
        jnp.where(low, a0, pltpu.roll(a3, 96, 1)),
        jnp.where(low, a1, pltpu.roll(a3, 64, 1)),
        jnp.where(low, a2, pltpu.roll(a3, 32, 1)),
    )


def fourth(t0, t1, t2):
    lane = lanes(t0.shape[0])
    return jnp.where(
        lane < 32,
        pltpu.roll(t0, 32, 1),
        jnp.where(lane < 64, pltpu.roll(t1, 64, 1), pltpu.roll(t2, 96, 1)),
    )


def dot(a, b):
    return jnp.dot(a, b, preferred_element_type=F32)


def fold_cells(m, cuts):
    last = m[cuts[3] : cuts[4]]
    out = []
    for g in range(3):
        here = m[cuts[g] : cuts[g + 1]]
        extra = here.shape[0] - last.shape[0]
        add = jnp.concatenate([last, jnp.zeros((extra, 128), F32)], axis=0) if extra else last
        out.append(jnp.where(lanes(here.shape[0]) < BS, here, pltpu.roll(add, 96 - 32 * g, 1)))
    return jnp.concatenate(out, axis=0).astype(BF16)


def unfold_cells(t, cuts):
    t = t.astype(F32)
    parts = [t[cuts[g] : cuts[g + 1]] for g in range(3)]
    n = cuts[4] - cuts[3]
    return jnp.concatenate(parts + [fourth(*(p[0:n] for p in parts))], axis=0)


def gelu(u):
    return 0.5 * u * (1.0 + lax.erf(u * (1.0 / math.sqrt(2.0))))


def kernel(
    lat_hbm,
    lon_hbm,
    x_hbm,
    sw1_hbm,
    sw2_hbm,
    ftab_hbm,
    gtab_hbm,
    ltab_hbm,
    w1_hbm,
    w2_hbm,
    out_hbm,
    kept_lat,
    kept_lon,
    x_ref,
    sw1,
    sw2,
    ftab,
    gtab,
    ltab,
    fmat,
    gmat,
    cs,
    ct,
    sf1,
    sf2,
    w1v,
    w2v,
    st_part,
    st_in,
    nrm,
    a_scr,
    f_send,
    f_recv,
    r_scr,
    b_scr,
    sp,
    b_send,
    b_recv,
    m_scr,
    c_send,
    c_recv,
    y_scr,
    n2,
    hid,
    d_send,
    d_recv,
    o_scr,
    o_buf,
    wsem,
    isem,
    osem,
    ssem,
    rsem,
):
    lat = lax.axis_index("lat")
    chan = lax.axis_index("chan")

    x_parts = [
        pl.ds(OUT_PAIRS[k] * W, (OUT_PAIRS[k + 1] - OUT_PAIRS[k]) * W) for k in range(NCH)
    ]
    x_loads = [
        pltpu.make_async_copy(x_hbm.at[part], x_ref.at[part], isem.at[k])
        for k, part in enumerate(x_parts)
    ]
    small = (
        (lat_hbm, kept_lat),
        (lon_hbm, kept_lon),
        (ftab_hbm, ftab),
        (gtab_hbm, gtab),
        (ltab_hbm, ltab),
        (sw1_hbm, sw1),
        (sw2_hbm, sw2),
    )
    s_loads = [
        pltpu.make_async_copy(src, dst, isem.at[NCH + i]) for i, (src, dst) in enumerate(small)
    ]
    loads = [
        pltpu.make_async_copy(w1_hbm, w1v, wsem.at[0]),
        pltpu.make_async_copy(w2_hbm, w2v, wsem.at[1]),
    ]
    for c in x_loads:
        c.start()

    barrier = pltpu.get_barrier_semaphore()

    def greet_lat(i, carry):
        pl.semaphore_signal(
            barrier, inc=1, device_id=(lax.rem(lat + i, L), chan), device_id_type=MESH
        )
        return carry

    def greet_chan(i, carry):
        pl.semaphore_signal(
            barrier, inc=1, device_id=(lat, lax.rem(chan + i, NC)), device_id_type=MESH
        )
        return carry

    lax.fori_loop(1, L, greet_lat, 0)
    lax.fori_loop(1, NC, greet_chan, 0)
    for c in s_loads + loads:
        c.start()

    def spread_lat(src, dst, phase, k, bounds):
        part = pl.ds(bounds[k], bounds[k + 1] - bounds[k])
        pltpu.make_async_copy(src.at[lat, part], dst.at[lat, part], rsem.at[phase, k]).start()

        def go(i, carry):
            to = lax.rem(lat + i, L)
            pltpu.make_async_remote_copy(
                src_ref=src.at[to, part],
                dst_ref=dst.at[lat, part],
                send_sem=ssem.at[phase, k],
                recv_sem=rsem.at[phase, k],
                device_id=(to, chan),
                device_id_type=MESH,
            ).start()
            return carry

        lax.fori_loop(1, L, go, 0)

    def arrived_lat(dst, phase, k, bounds):
        part = dst.at[pl.ds(0, L), pl.ds(bounds[k], bounds[k + 1] - bounds[k])]
        pltpu.make_async_copy(part, part, rsem.at[phase, k]).wait()
        for s in range(L):
            for b in range(bounds[k], bounds[k + 1]):
                r_scr[pl.ds((s * NB + b) * 8, 8), :] = dst[s, b].astype(F32)

    def sent_lat(dst, phase, k, bounds):
        part = dst.at[pl.ds(0, L - 1), pl.ds(bounds[k], bounds[k + 1] - bounds[k])]
        pltpu.make_async_copy(part, part, ssem.at[phase, k]).wait()

    def regroup(dst, k, bounds):
        for d in range(L):
            for b in range(bounds[k], bounds[k + 1]):
                dst[d, b] = a_scr[pl.ds(b * 256 + d, 8, stride=32), :].astype(BF16)

    def spread_chan(src, dst, phase, k, rows, same):
        part = pl.ds(0, rows)
        own = src.at[k, 0 if same else chan, part]
        pltpu.make_async_copy(own, dst.at[k, chan, part], rsem.at[phase, k]).start()

        def go(i, carry):
            to = lax.rem(chan + i, NC)
            pltpu.make_async_remote_copy(
                src_ref=src.at[k, 0 if same else to, part],
                dst_ref=dst.at[k, chan, part],
                send_sem=ssem.at[phase, k],
                recv_sem=rsem.at[phase, k],
                device_id=(lat, to),
                device_id_type=MESH,
            ).start()
            return carry

        lax.fori_loop(1, NC, go, 0)

    def arrived(dst, phase, k, count, rows):
        part = dst.at[k, pl.ds(0, count), pl.ds(0, rows)]
        pltpu.make_async_copy(part, part, rsem.at[phase, k]).wait()

    def sent(dst, phase, k, count, rows):
        part = dst.at[k, pl.ds(0, count), pl.ds(0, rows)]
        pltpu.make_async_copy(part, part, ssem.at[phase, k]).wait()

    lane = lax.broadcasted_iota(jnp.int32, (BS, 128), 1)
    left = jnp.where(lane < TH, 1.0, 0.0).astype(BF16)
    right = jnp.where(lane >= TH, 1.0, 0.0).astype(BF16)
    own_lane = lax.rem(lanes(TH), TH) == lax.broadcasted_iota(jnp.int32, (TH, 128), 0)
    st_part[...] = jnp.zeros_like(st_part)
    for k in range(NCH):
        x_loads[k].wait()
        for g in range(OUT_PAIRS[k], OUT_PAIRS[k + 1]):
            xr = x_ref[pl.ds(g * W, W), :]
            xf = xr.astype(F32)
            sq = xf * xf
            hi = sq.astype(BF16)
            lo = (sq - hi.astype(F32)).astype(BF16)
            sums = dot(xr, left) + dot(hi, right) + dot(lo, right)
            for j in range(TR):
                row = jnp.where(own_lane, sums[j * TH : (j + 1) * TH], 0.0)
                st_part[k, 0, pl.ds((g - OUT_PAIRS[k]) * TR + j, 1), :] = jnp.sum(row, axis=0, keepdims=True)
        if k == 0:
            pl.semaphore_wait(barrier, L - 1 + NC - 1)
        spread_chan(st_part, st_in, 0, k, STAT_ROWS[k], True)

    for c in s_loads:
        c.wait()
    nrm[...] = jnp.zeros_like(nrm)
    a_scr[pl.ds(NG * 96, 64), :] = jnp.zeros((64, 128), F32)
    for q in range(4):
        for b in range(2):
            blk = kept_lon[(q // 2) * 2 + b]
            fmat[pl.ds(q * 32 + b * 16, 16), :] = ftab[q % 2, blk]
    g = jnp.concatenate(
        [gtab[q % 2, kept_lon[(q // 2) * 2 + b]].astype(F32) for q in range(4) for b in range(2)],
        axis=0,
    )
    gmat[...] = g.T[0:W].astype(BF16)
    t = jnp.concatenate([ltab[q, kept_lat[b]].astype(F32) for q in range(2) for b in range(4)], axis=0)
    cs[...] = t.astype(BF16)
    ct[...] = t.T[0:H].astype(BF16)
    for src, dst in ((sw1, sf1), (sw2, sf2)):
        dst[...] = jnp.zeros_like(dst)
        real, imag = src[0], src[1]
        dst[pl.ds(0, BS), pl.ds(0, BS)] = real
        dst[pl.ds(0, BS), pl.ds(128, BS)] = imag
        dst[pl.ds(128, BS), pl.ds(0, BS)] = -imag
        dst[pl.ds(128, BS), pl.ds(128, BS)] = real

    for k in range(NCH):
        arrived(st_in, 0, k, NC, STAT_ROWS[k])
        rows = pl.ds(0, STAT_ROWS[k])
        tot = st_in[k, 0, rows, :]
        for i in range(1, NC):
            tot = tot + st_in[k, i, rows, :]
        tot = tot * (1.0 / C)
        var = pltpu.roll(tot, TH, 1) - tot * tot
        scale = pltpu.roll(lax.rsqrt(var + EPS), TH, 1)
        stat = jnp.where(lanes(STAT_ROWS[k]) < TH, tot, scale).T
        pairs = range(OUT_PAIRS[k], OUT_PAIRS[k + 1])
        for i in range(len(pairs) * TR):
            part = pl.ds(pairs[0] * W + i * TH, TH)
            xf = x_ref[part, :].astype(F32)
            normed = (xf - stat[0:TH, i : i + 1]) * stat[TH : 2 * TH, i : i + 1]
            nrm[part, pl.ds(0, BS)] = normed.astype(BF16)
        side = [nrm[pl.ds(g * W, W), :] for g in pairs]
        al = dot(fmat[...], jnp.concatenate(side, axis=1))
        for r, g in enumerate(pairs):
            parts = fold(*(al[q * 32 : (q + 1) * 32, r * 128 : (r + 1) * 128] for q in range(4)))
            for p in range(3):
                a_scr[pl.ds((g * 3 + p) * 32, 32), :] = parts[p]
        regroup(f_send, k, OUT_BLOCKS)
        spread_lat(f_send, f_recv, 1, k, OUT_BLOCKS)

    for k in range(NCH):
        arrived_lat(f_recv, 1, k, OUT_BLOCKS)
        for n in range(SC):
            for hh in range(RH):
                for p in range(3):
                    row = ((k * SC + n) * RH + hh) * 3 + p
                    b_scr[pl.ds(hh * 32, 32), pl.ds((n * 3 + p) * 128, 128)] = r_scr[
                        pl.ds(row, 32, stride=NB * 8), :
                    ].astype(BF16)
        both = dot(cs[:, 0:H], b_scr[...])
        for n in range(SC):
            cols = [slice((n * 3 + p) * 128, (n * 3 + p + 1) * 128) for p in range(3)]
            co = [both[0:64, c] for c in cols]
            si = [both[64:128, c] for c in cols]
            co.append(fourth(*co))
            si.append(fourth(*si))
            for m in range(2):
                rows = pl.ds((n * 2 + m) * 64, 64)
                sp[rows, pl.ds(0, 128)] = (co[2 * m] + si[2 * m + 1]).astype(BF16)
                sp[rows, pl.ds(128, 128)] = (co[2 * m + 1] - si[2 * m]).astype(BF16)
        one = jnp.maximum(dot(sp[...], sf1[...]), 0.0).astype(BF16)
        two = dot(one, sf2[...]).astype(BF16)
        side = []
        for i in range(SC * 2):
            f = two[i * 64 : (i + 1) * 64]
            turned = jnp.concatenate([-f[:, 128:256], f[:, 0:128]], axis=1)
            side.append(jnp.concatenate([f, turned], axis=0))
        wave = dot(ct[...], jnp.concatenate(side, axis=1))
        for n in range(SC):
            parts = fold(*(wave[:, (n * 4 + q) * 128 : (n * 4 + q + 1) * 128] for q in range(4)))
            for hh in range(RH):
                for p in range(3):
                    row = ((k * SC + n) * RH + hh) * 3 + p
                    a_scr[pl.ds(row * 32, 32), :] = parts[p][hh * 32 : (hh + 1) * 32]
        regroup(b_send, k, BACK_BLOCKS)
        spread_lat(b_send, b_recv, 2, k, BACK_BLOCKS)

    for k in range(NCH):
        arrived_lat(b_recv, 2, k, BACK_BLOCKS)
        pairs = range(BACK_PAIRS[k], BACK_PAIRS[k + 1])
        side = []
        for g in pairs:
            parts = [r_scr[pl.ds(g * 3 + p, 32, stride=NB * 8), :] for p in range(3)]
            side.append(jnp.concatenate(parts + [fourth(*parts)], axis=0).astype(BF16))
        spectral = dot(gmat[...], jnp.concatenate(side, axis=1))
        for r, g in enumerate(pairs):
            at = pl.ds(g * W, W)
            mixed = x_ref[at, :].astype(F32) + nrm[at, pl.ds(0, BS)].astype(F32)
            mixed = mixed + spectral[:, r * 128 : r * 128 + BS]
            j = sum(g >= v for v in BOUNDS[1:])
            for d in range(NC):
                m_scr[d, pl.ds(g * WS, WS), pl.ds(0, BS)] = mixed[d * WS : (d + 1) * WS]
            if g == BOUNDS[j + 1] - 1:
                for d in range(NC):
                    c_send[j, d, pl.ds(0, PACKED[j]), :] = fold_cells(
                        m_scr[d, pl.ds(BOUNDS[j] * WS, ROWS[j] * WS), :], CUTS[ROWS[j]]
                    )
                spread_chan(c_send, c_recv, 3, j, PACKED[j], False)

    for c in loads:
        c.wait()
    for k in range(NT):
        arrived(c_recv, 3, k, NC, PACKED[k])
        cuts = CUTS[ROWS[k]]
        cells = ROWS[k] * WS
        lane = lanes(cells)
        acc = jnp.zeros((cells, 128), F32)
        acc2 = jnp.zeros((cells, 128), F32)
        for s in range(NC):
            y = unfold_cells(c_recv[k, s, pl.ds(0, PACKED[k]), :], cuts)
            y = jnp.where(lane < BS, y, 0.0)
            y_scr[s, pl.ds(0, cells), :] = y
            acc = acc + y
            acc2 = acc2 + y * y
        mean = jnp.sum(acc, axis=1, keepdims=True) * (1.0 / C)
        var = jnp.sum(acc2, axis=1, keepdims=True) * (1.0 / C) - mean * mean
        scale = lax.rsqrt(var + EPS)
        for i in range(2):
            z = [(y_scr[4 * i + j, pl.ds(0, cells), :] - mean) * scale for j in range(4)]
            z = [z[0]] + [pltpu.roll(z[j], 128 - 32 * j, 1) for j in range(1, 4)]
            for j in range(3):
                tile = jnp.where(lane < BS - 32 * j, z[j], z[j + 1])
                n2[pl.ds(0, cells), pl.ds((3 * i + j) * 128, 128)] = tile.astype(BF16)
        n2k = n2[pl.ds(0, cells), :]
        for i in range(HID // 512):
            cols = pl.ds(i * 512, 512)
            hid[pl.ds(0, cells), cols] = gelu(dot(n2k, w1v[:, cols])).astype(BF16)
        o = dot(hid[pl.ds(0, cells), :], w2v[...])
        tiles = [o[:, i * 128 : (i + 1) * 128] for i in range(6)]
        for s in range(NC):
            i, off = divmod(s * BS, 128)
            piece = tiles[i]
            if off:
                piece = pltpu.roll(piece, 128 - off, 1)
                if off > 32:
                    after = pltpu.roll(tiles[i + 1], 128 - off, 1)
                    piece = jnp.where(lane < 128 - off, piece, after)
            d_send[k, s, pl.ds(0, PACKED[k]), :] = fold_cells(
                y_scr[s, pl.ds(0, cells), :] + piece, cuts
            )
        spread_chan(d_send, d_recv, 4, k, PACKED[k], False)

    stores = []
    for k in range(NT):
        arrived(d_recv, 4, k, NC, PACKED[k])
        for s in range(NC):
            y = unfold_cells(d_recv[k, s, pl.ds(0, PACKED[k]), :], CUTS[ROWS[k]])
            for r in range(ROWS[k]):
                o_scr[pl.ds(r * W + s * WS, WS), :] = y[r * WS : (r + 1) * WS]
        at = pl.ds(BOUNDS[k] * W, ROWS[k] * W)
        o_buf[at, :] = o_scr[pl.ds(0, ROWS[k] * W), :].astype(BF16)
        stores.append(pltpu.make_async_copy(o_buf.at[at], out_hbm.at[at], osem.at[k]))
        stores[k].start()
    for c in stores:
        c.wait()
    for k in range(NCH):
        sent(st_in, 0, k, NC - 1, STAT_ROWS[k])
        sent_lat(f_send, 1, k, OUT_BLOCKS)
        sent_lat(b_send, 2, k, BACK_BLOCKS)
    for k in range(NT):
        sent(c_send, 3, k, NC - 1, PACKED[k])
        sent(d_send, 4, k, NC - 1, PACKED[k])


def hand_on(i_ref, o_ref, buf, narrow, sem_in, sem_out):
    step = i_ref.shape[0] // 6
    parts = [pl.ds(i * step, step) for i in range(6)]
    reads = [pltpu.make_async_copy(i_ref.at[p], buf.at[p], sem_in.at[i]) for i, p in enumerate(parts)]
    writes = [pltpu.make_async_copy(narrow.at[p], o_ref.at[p], sem_out.at[i]) for i, p in enumerate(parts)]
    for c in reads:
        c.start()
    for p, r, w in zip(parts, reads, writes):
        r.wait()
        narrow[p, :] = buf[p, 0:BS]
        w.start()
    for c in writes:
        c.wait()


def on_device(fields, kept_lat, kept_lon, spec_w1, spec_w2, mlp_w1, mlp_w2):
    fwd, inv, lat = tables()
    hbm = pl.BlockSpec(memory_space=pltpu.HBM)
    cells = S * RH * W
    parts = pl.pallas_call(
        kernel,
        out_shape=jax.ShapeDtypeStruct((cells, 128), BF16),
        in_specs=[hbm] * 10,
        out_specs=hbm,
        scratch_shapes=[
            pltpu.SMEM((4,), jnp.int32),
            pltpu.SMEM((4,), jnp.int32),
            pltpu.VMEM((cells, BS), BF16),
            pltpu.VMEM((2, BS, BS), BF16),
            pltpu.VMEM((2, BS, BS), BF16),
            pltpu.VMEM(fwd.shape, BF16),
            pltpu.VMEM(inv.shape, BF16),
            pltpu.VMEM(lat.shape, BF16),
            pltpu.VMEM((128, W), BF16),
            pltpu.VMEM((W, 128), BF16),
            pltpu.VMEM((128, 128), BF16),
            pltpu.VMEM((H, 128), BF16),
            pltpu.VMEM((256, 256), BF16),
            pltpu.VMEM((256, 256), BF16),
            pltpu.VMEM((C, HID), BF16),
            pltpu.VMEM((HID, C), BF16),
            pltpu.VMEM((NCH, 1, STAT_ROWS[0], 128), F32),
            pltpu.VMEM((NCH, NC, STAT_ROWS[0], 128), F32),
            pltpu.VMEM((cells, 128), BF16),
            pltpu.VMEM((NB * 256, 128), F32),
            pltpu.VMEM((L, NB, 8, 128), BF16),
            pltpu.VMEM((L, NB, 8, 128), BF16),
            pltpu.VMEM((NB * 256, 128), F32),
            pltpu.VMEM((H, SC * 384), BF16),
            pltpu.VMEM((SC * 128, 256), BF16),
            pltpu.VMEM((L, NB, 8, 128), BF16),
            pltpu.VMEM((L, NB, 8, 128), BF16),
            pltpu.VMEM((NC, S * RH * WS, 128), F32),
            pltpu.VMEM((NT, NC, MAXP, 128), BF16),
            pltpu.VMEM((NT, NC, MAXP, 128), BF16),
            pltpu.VMEM((NC, MAXC, 128), F32),
            pltpu.VMEM((MAXC, C), BF16),
            pltpu.VMEM((MAXC, HID), BF16),
            pltpu.VMEM((NT, NC, MAXP, 128), BF16),
            pltpu.VMEM((NT, NC, MAXP, 128), BF16),
            pltpu.VMEM((max(ROWS) * W, 128), F32),
            pltpu.VMEM((cells, 128), BF16),
            pltpu.SemaphoreType.DMA((2,)),
            pltpu.SemaphoreType.DMA((NCH + 7,)),
            pltpu.SemaphoreType.DMA((NT,)),
            pltpu.SemaphoreType.DMA((5, NT)),
            pltpu.SemaphoreType.DMA((5, NT)),
        ],
        compiler_params=pltpu.CompilerParams(
            collective_id=0, has_side_effects=True, vmem_limit_bytes=56 * 1024 * 1024
        ),
        cost_estimate=pl.CostEstimate(
            flops=5_000_000_000, bytes_accessed=12_000_000, transcendentals=1_400_000
        ),
    )(
        kept_lat,
        kept_lon,
        fields.reshape(cells, BS),
        spec_w1.reshape(2, BS, BS),
        spec_w2.reshape(2, BS, BS),
        fwd,
        inv,
        lat,
        mlp_w1,
        mlp_w2,
    )
    out = pl.pallas_call(
        hand_on,
        out_shape=jax.ShapeDtypeStruct((cells, BS), BF16),
        in_specs=[pl.BlockSpec(memory_space=pltpu.HBM)],
        out_specs=pl.BlockSpec(memory_space=pltpu.HBM),
        scratch_shapes=[
            pltpu.VMEM((cells, 128), BF16),
            pltpu.VMEM((cells, BS), BF16),
            pltpu.SemaphoreType.DMA((6,)),
            pltpu.SemaphoreType.DMA((6,)),
        ],
    )(parts)
    return out.reshape(S, RH, W, BS)


def solution(mesh):
    placed = (
        P(None, "lat", None, "chan"),
        P(),
        P(),
        P(None, "chan", None, None),
        P(None, "chan", None, None),
        P(),
        P(),
    )
    return jax.shard_map(
        on_device,
        mesh=mesh,
        in_specs=placed,
        out_specs=P(None, "lat", None, "chan"),
        check_vma=False,
    )
```
